256 devices in a mesh: panel: 32 (over z_hi, y, core), tile: 8 (over z_lo, x).
Axes of the slice: x: 4, y: 4, z: 8 (z_hi: 4, z_lo: 2; z = z_hi * 2 + z_lo), core: 2. Of those that a mesh axis runs over, the one named last changes fastest.
Arguments:
- velocity: bfloat16 [4096, 3, 2, 4096], P('tile', None, None, 'panel'), may hold values from -6 to 6
- elevation: bfloat16 [4096, 2, 4096], P('tile', None, 'panel'), may hold values from -6 to 6
- panel_area: float32 [4096], P('panel'), may hold values from 0.5 to 2
- normal: float32 [4096], P('panel'), may hold values from -1 to 1
- block_map: int32 [4096], P('panel'), may hold values from 0 to 15
- waterline: int32 [4096], P('panel'), may hold values 0 or 1
- heading: int32 [4096], replicated, may hold values from 0 to 7
- section: float32 [16], replicated, may hold values from 0.5 to 2
- heading_table: float32 [8, 8], replicated, may hold values from 0.5 to 1.5
Outputs:
- qtf: float32 [4096, 2, 4096], P('panel', None, 'tile')
The draws below stay inside these ranges and needn't reach their ends.
All inputs are finite; a program needn't handle non-finite values. No bound on the sum of `waterline` on one device may be relied on, other than what follows from the above.
Results may differ from the reference program's by a relative error of at most 0.0003.
Values may be sent and summed in bfloat16 or wider, within the bound.
A program may use at most 128 MiB of HBM per device.

```python
import math
import jax
import jax.numpy as jnp
from jax import lax

NC = 4096
NB = 16
NH = 8
NPANEL = 4096


def set_ends(drawn, key, low, top_value):
    index_at = [jax.random.randint(jax.random.fold_in(key, axis), (), 0, length) for axis, length in enumerate(drawn.shape)]
    widest = drawn.shape.index(max(drawn.shape))
    beside = index_at[:widest] + [(index_at[widest] + 1) % drawn.shape[widest]] + index_at[widest + 1:]
    return drawn.at[tuple(index_at)].set(low).at[tuple(beside)].set(top_value)


def block_scale(stream_key, shape, split, smallest, high):
    def one(dim, shards_of):
        draws = jax.random.uniform(jax.random.fold_in(jax.random.fold_in(stream_key, 6), dim), (shards_of,), jnp.float32, smallest / len(split), high / len(split))
        return jnp.repeat(jnp.exp(draws), shape[dim] // shards_of).reshape((-1,) + (1,) * (len(shape) - dim - 1))

    level = one(*split[0])
    for cut in split[1:]:
        level = level * one(*cut)
    return level


def noise(key, extent, scale, bound, split=(), kind=jnp.bfloat16):
    entries = scale * jax.random.normal(key, extent, jnp.float32)
    if split:
        entries = entries * block_scale(key, extent, split, -0.22, 0.18)
    return jnp.clip(entries, -bound, bound).astype(kind)


def setup_inputs(seed: int = 0) -> dict:
    seeds = jax.random.split(jax.random.key(seed), 10)
    velocity = noise(seeds[0], (NC, 3, 2, NPANEL), 1.0, 6.0, ((0, 8), (3, 32)))
    elevation = noise(seeds[1], (NC, 2, NPANEL), 1.0, 6.0, ((0, 8), (2, 32)))
    panel_area = jnp.clip(jnp.exp(math.log(2.0) - 1.3862944 * jax.random.uniform(seeds[2], (NPANEL,), jnp.float32) ** block_scale(seeds[2], (NPANEL,), ((0, 32),), -0.2, 0.2)), 0.5, 2.0)
    normal = jnp.clip(jax.random.uniform(seeds[3], (NPANEL,), jnp.float32, -1.0, 1.0) * block_scale(seeds[3], (NPANEL,), ((0, 32),), -0.4, 0.0), -1.0, 1.0)
    block_map = set_ends(jax.random.randint(seeds[4], (NPANEL,), 0, NB), jax.random.fold_in(seeds[4], 1), 0, NB - 1).astype(jnp.int32)
    waterline = set_ends((jax.random.randint(seeds[5], (NPANEL,), 0, 2) < 1).astype(jnp.int32), jax.random.fold_in(seeds[5], 1), 0, 1)
    heading = set_ends(jax.random.randint(seeds[6], (NC,), 0, NH), jax.random.fold_in(seeds[6], 1), 0, NH - 1).astype(jnp.int32)
    section = jnp.clip(jnp.exp(jax.random.uniform(seeds[7], (NB,), jnp.float32, math.log(0.5), math.log(2.0))), 0.5, 2.0)
    heading_table = jnp.clip(jax.random.uniform(seeds[8], (NH, NH), jnp.float32, 0.5, 1.5), 0.5, 1.5)
    return {"velocity": velocity, "elevation": elevation, "panel_area": panel_area, "normal": normal, "block_map": block_map, "waterline": waterline, "heading": heading, "section": section, "heading_table": heading_table}


def panel_weights(panel_area, normal, block_map, waterline, section, norm_scale):
    sections = jnp.arange(section.shape[0], dtype=jnp.int32)
    section_gain = lax.optimization_barrier(jnp.sum(jnp.where(block_map[None, :] == sections[:, None], section[:, None], jnp.zeros_like(section[:, None])), axis=0))
    mode_value = normal * section_gain * norm_scale
    pressure = -0.5 * panel_area * mode_value
    water_line = 0.5 * waterline.astype(jnp.float32) * mode_value
    return jnp.stack([pressure, pressure, pressure, water_line], axis=0)

def weighted_side(fields, weights):
    direct = fields.astype(jnp.float32) * weights[None, :, None, :]
    rotated = jnp.stack([-direct[:, :, 1], direct[:, :, 0]], axis=2)
    return jnp.stack([direct, rotated], axis=0)

def reference(velocity, elevation, panel_area, normal, block_map, waterline, heading, section, heading_table):
    fields = jnp.concatenate([velocity, elevation[:, None]], axis=1)
    weights = panel_weights(panel_area, normal, block_map, waterline, section, 1.0 / math.sqrt(NPANEL))
    right_side = weighted_side(fields, weights).reshape(2 * NC, -1)
    left_side = fields.reshape(NC, -1).astype(jnp.float32)
    summed = lax.dot_general(left_side, right_side, (((1,), (1,)), ((), ())), precision=lax.Precision.HIGHEST, preferred_element_type=jnp.float32)
    summed = summed.reshape(NC, 2, NC)
    factor = heading_table[heading[:, None], heading[None, :]]
    return summed * factor[:, None, :]
```

```python
import functools
import math

import jax
import jax.numpy as jnp
from jax import lax
from jax.experimental import pallas as pl
from jax.experimental.pallas import tpu as pltpu
from jax.sharding import PartitionSpec as P

MESH = pl.DeviceIdType.MESH
ROWS = 512
DEPTH = 1024
COLS = 1024
BLOCK = 128
LEVELS = 32000.0


def panel_weights(panel_area, normal, block_map, waterline, section, norm_scale):
    sections = jnp.arange(section.shape[0], dtype=jnp.int32)
    section_gain = jnp.sum(
        jnp.where(
            block_map[None, :] == sections[:, None],
            section[:, None],
            jnp.zeros_like(section[:, None]),
        ),
        axis=0,
    )
    mode_value = normal * section_gain * norm_scale
    pressure = -0.5 * panel_area * mode_value
    water_line = 0.5 * waterline.astype(jnp.float32) * mode_value
    return jnp.stack([pressure, pressure, pressure, water_line], axis=0)


def quantize(value):
    tiles = value.reshape(BLOCK // 8, 8, COLS)
    top = jnp.max(jnp.abs(tiles), axis=0)
    peak = top[:, :128]
    for k in range(1, COLS // 128):
        peak = jnp.maximum(peak, top[:, k * 128 : (k + 1) * 128])
    peak = jnp.maximum(peak, 1e-30)
    inverse = jnp.concatenate([LEVELS / peak] * (COLS // 128), axis=1)
    scaled = jnp.round(tiles * inverse[None]).astype(jnp.int32)
    return scaled.reshape(BLOCK, COLS).astype(jnp.int16), peak * (1.0 / LEVELS)


def dequantize(coded, scale):
    wide = jnp.concatenate([scale] * (COLS // 128), axis=1)
    tiles = coded.astype(jnp.int32).astype(jnp.float32).reshape(BLOCK // 8, 8, COLS)
    return (tiles * wide[None]).reshape(BLOCK, COLS)


def kernel(
    field_ref, weight_ref, out_ref,
    held, across, own_hi, own_lo, across_hi, across_lo, part, core_in,
    y_out, y_out_scale, y_in, y_in_scale, z_out, z_out_scale, z_in, z_in_scale,
    total, mirror_in,
    g_send, g_recv, c_send, c_recv, y_send, y_recv, z_send, z_recv, m_send, m_recv,
):
    panel, tile = lax.axis_index("panel"), lax.axis_index("tile")
    zh, y, c = panel // 8, (panel // 2) % 4, panel % 2
    a, x = tile // 4, tile % 4

    def at(zh_, y_, c_, a_, x_):
        return (zh_ * 8 + y_ * 2 + c_, a_ * 4 + x_)

    def copy(src, dst, send, recv, device):
        return pltpu.make_async_remote_copy(
            src_ref=src, dst_ref=dst, send_sem=send, recv_sem=recv, device_id=device, device_id_type=MESH
        )

    shifts = (0, 1, 2, 2 * a, 1)
    odd = (0, 1, 0, 0, 1)
    crossed = (False, False, False, True, True)

    row_tile = panel // 4
    row_a, row_x = row_tile // 4, row_tile % 4
    shift = (row_x - x + 4) % 4
    is_own = jnp.logical_and(row_a == a, shift < 3)
    is_cross = jnp.logical_and(row_a != a, jnp.logical_or(shift == 1, shift == 2 * row_a))
    is_direct = jnp.logical_or(is_own, is_cross)
    gives = jnp.logical_or(is_cross, jnp.logical_and(row_a == a, shift == 1))
    off_diagonal = row_tile != tile

    core_mate = at(zh, y, 1 - c, a, x)
    z_mate = at(zh, y, c, 1 - a, x)
    x_mates = [at(zh, y, c, a, (x + k) % 4) for k in (1, 2, 3)]
    y_mates = [at(zh, (y + k) % 4, c, a, x) for k in (1, 2, 3)]
    zh_mates = [at((zh + k) % 4, y, c, a, x) for k in (1, 2, 3)]
    far_mates = [at((zh + k) % 4, y, c, 1 - a, x) for k in (1, 2, 3)]
    mirrors = [(tile * 4 + q, row_tile) for q in range(4)]

    barrier = pltpu.get_barrier_semaphore()
    always = [core_mate, z_mate] + x_mates + y_mates + zh_mates + far_mates
    for mate in always:
        pl.semaphore_signal(barrier, inc=1, device_id=mate, device_id_type=MESH)

    @pl.when(off_diagonal)
    def _():
        for mate in mirrors:
            pl.semaphore_signal(barrier, inc=1, device_id=mate, device_id_type=MESH)
        pl.semaphore_wait(barrier, len(always) + len(mirrors))

    @pl.when(jnp.logical_not(off_diagonal))
    def _():
        pl.semaphore_wait(barrier, len(always))

    gathers = [
        copy(field_ref, held.at[1], g_send.at[0], g_recv.at[0], x_mates[2]),
        copy(field_ref, held.at[2], g_send.at[1], g_recv.at[1], x_mates[1]),
        copy(field_ref, across, g_send.at[2], g_recv.at[2], z_mate),
    ]
    for gather in gathers:
        gather.start()

    def right_side(src, hi, lo):
        @pl.loop(0, 4)
        def _(q):
            rows = pl.ds(pl.multiple_of(q * BLOCK, BLOCK), BLOCK)
            direct = pl.ds(pl.multiple_of(q * 2 * BLOCK, BLOCK), BLOCK)
            rotated = pl.ds(pl.multiple_of(q * 2 * BLOCK + BLOCK, BLOCK), BLOCK)
            for k in range(DEPTH // 128):
                lanes = pl.ds(k * 128, 128)
                turned = pl.ds((k ^ 1) * 128, 128)
                value = src[rows, lanes].astype(jnp.float32) * weight_ref[:, lanes]
                high = value.astype(jnp.bfloat16)
                low = (value - high.astype(jnp.float32)).astype(jnp.bfloat16)
                hi[direct, lanes] = high
                lo[direct, lanes] = low
                hi[rotated, turned] = high if k % 2 == 0 else -high
                lo[rotated, turned] = low if k % 2 == 0 else -low

    def product(p, left, hi, lo):
        @pl.loop(0, 4)
        def _(k):
            columns = pl.ds(pl.multiple_of(k * 256, 256), 256)
            for r in range(2):
                rows = pl.ds(r * 256, 256)
                value = lax.dot_general(
                    left[rows, :], hi[columns, :], (((1,), (1,)), ((), ())), preferred_element_type=jnp.float32
                )
                value += lax.dot_general(
                    left[rows, :], lo[columns, :], (((1,), (1,)), ((), ())), preferred_element_type=jnp.float32
                )
                part[p, rows, columns] = value

    def core_copies(p):
        out = []
        for low in range(2):
            rows = pl.ds(pl.multiple_of((1 - c) * BLOCK + low * 2 * BLOCK, BLOCK), BLOCK)
            out.append(
                copy(part.at[p, rows], core_in.at[p, low], c_send.at[p, low], c_recv.at[p, low], core_mate)
            )
        return out

    def mine(p, low):
        return pl.ds(pl.multiple_of(c * BLOCK + low * 2 * BLOCK, BLOCK), BLOCK)

    def y_half(p):
        return (x + odd[p]) % 2

    def y_copies(p, low):
        target = y_half(p) * 2 + low
        slot = (y - target + 4) % 4 - 1
        device = at(zh, target, c, a, x)
        return [
            copy(y_out.at[p, low], y_in.at[p, slot], y_send.at[p, low, 0], y_recv.at[p, slot, 0], device),
            copy(y_out_scale.at[p, low], y_in_scale.at[p, slot], y_send.at[p, low, 1], y_recv.at[p, slot, 1], device),
        ]

    def start_core(p):
        for item in core_copies(p):
            item.start()

    def start_y(p):
        for low, item in enumerate(core_copies(p)):
            item.wait_recv()
            value = part[p, mine(p, low), :] + core_in[p, low]
            local = y_half(p) * 2 + low == y

            @pl.when(local)
            def _(value=value, low=low):
                part[p, mine(p, low), :] = value

            @pl.when(jnp.logical_not(local))
            def _(value=value, low=low):
                y_out[p, low], y_out_scale[p, low] = quantize(value)
                for each in y_copies(p, low):
                    each.start()

    def z_target(p):
        return a * 2 + ((x + shifts[p]) % 4) // 2

    def z_copies(p):
        device = at(z_target(p), y, c, 1 - a if crossed[p] else a, x)
        return [
            copy(z_out.at[p], z_in.at[zh], z_send.at[p, 0], z_recv.at[zh, 0], device),
            copy(z_out_scale.at[p], z_in_scale.at[zh], z_send.at[p, 1], z_recv.at[zh, 1], device),
        ]

    def start_z(p):
        @pl.when(y_half(p) == y // 2)
        def _():
            low = y % 2
            value = part[p, mine(p, low), :]
            for slot in range(3):
                for k, (src, dst) in enumerate(
                    ((y_out.at[p, 0], y_in.at[p, slot]), (y_out_scale.at[p, 0], y_in_scale.at[p, slot]))
                ):
                    copy(src, dst, y_send.at[p, 0, k], y_recv.at[p, slot, k], y_mates[0]).wait_recv()
                value += dequantize(y_in[p, slot], y_in_scale[p, slot])

            def send():
                z_out[p], z_out_scale[p] = quantize(value)
                for each in z_copies(p):
                    each.start()

            if crossed[p]:
                send()
            else:
                local = z_target(p) == zh

                @pl.when(local)
                def _():
                    total[...] = value

                @pl.when(jnp.logical_not(local))
                def _():
                    send()

    right_side(field_ref, own_hi, own_lo)
    product(0, field_ref, own_hi, own_lo)
    start_core(0)
    held[0] = field_ref[...]
    start_y(0)
    gathers[0].wait_recv()
    product(1, held.at[1], own_hi, own_lo)
    start_core(1)
    gathers[2].wait_recv()
    right_side(across, across_hi, across_lo)
    start_y(1)
    product(4, held.at[1], across_hi, across_lo)
    start_core(4)
    start_z(0)
    start_y(4)
    gathers[1].wait_recv()
    product(2, held.at[2], own_hi, own_lo)
    start_core(2)
    product(3, held.at[2 * a], across_hi, across_lo)
    start_core(3)
    start_y(2)
    start_y(3)
    start_z(1)
    start_z(4)
    start_z(2)
    start_z(3)

    def wait_z(source):
        for k, (src, dst) in enumerate(((z_out.at[0], z_in.at[source]), (z_out_scale.at[0], z_in_scale.at[source]))):
            copy(src, dst, z_send.at[0, k], z_recv.at[source, k], zh_mates[0]).wait_recv()

    @pl.when(is_own)
    def _():
        for k in range(1, 4):
            source = (zh + k) % 4
            wait_z(source)
            total[...] += dequantize(z_in[source], z_in_scale[source])

    @pl.when(is_cross)
    def _():
        for source in range(4):
            wait_z(source)
            value = dequantize(z_in[source], z_in_scale[source])
            total[...] = value if source == 0 else total[...] + value

    def mirror_copies():
        slot = panel % 4
        return [
            copy(
                total.at[:, pl.ds(q * 256, 256)], mirror_in.at[slot], m_send.at[q], m_recv.at[slot], mirrors[q]
            )
            for q in range(4)
        ]

    @pl.when(gives)
    def _():
        for each in mirror_copies():
            each.start()

    @pl.when(is_direct)
    def _():
        for q in range(4):
            out_ref[:, q * 128 : (q + 1) * 128] = total[:, q * 256 : q * 256 + 128]
            out_ref[:, 512 + q * 128 : 512 + (q + 1) * 128] = total[:, q * 256 + 128 : (q + 1) * 256]

    @pl.when(jnp.logical_not(is_direct))
    def _():
        for q in range(4):
            copy(
                total.at[:, pl.ds(q * 256, 256)], mirror_in.at[q], m_send.at[q], m_recv.at[q], mirrors[q]
            ).wait_recv()
            out_ref[:, q * 128 : (q + 1) * 128] = mirror_in[q, :, :128].T
            out_ref[:, 512 + q * 128 : 512 + (q + 1) * 128] = -mirror_in[q, :, 128:].T

    for gather in gathers:
        gather.wait_send()
    for p in range(5):
        for low, item in enumerate(core_copies(p)):
            item.wait_send()

            @pl.when(y_half(p) * 2 + low != y)
            def _(p=p, low=low):
                for each in y_copies(p, low):
                    each.wait_send()

        sends = y_half(p) == y // 2
        if not crossed[p]:
            sends = jnp.logical_and(sends, z_target(p) != zh)

        @pl.when(sends)
        def _(p=p):
            for each in z_copies(p):
                each.wait_send()

    @pl.when(gives)
    def _():
        for each in mirror_copies():
            each.wait_send()


def reduced_product(fields, weights):
    vmem, f32, bf16, i16 = pltpu.VMEM, jnp.float32, jnp.bfloat16, jnp.int16
    dma = pltpu.SemaphoreType.DMA
    return pl.pallas_call(
        kernel,
        out_shape=jax.ShapeDtypeStruct((BLOCK, COLS), f32),
        in_specs=[pl.BlockSpec(memory_space=vmem)] * 2,
        out_specs=pl.BlockSpec(memory_space=vmem),
        scratch_shapes=[
            vmem((3, ROWS, DEPTH), bf16), vmem((ROWS, DEPTH), bf16),
            vmem((COLS, DEPTH), bf16), vmem((COLS, DEPTH), bf16),
            vmem((COLS, DEPTH), bf16), vmem((COLS, DEPTH), bf16),
            vmem((5, ROWS, COLS), f32), vmem((5, 2, BLOCK, COLS), f32),
            vmem((5, 2, BLOCK, COLS), i16), vmem((5, 2, 8, 128), f32),
            vmem((5, 3, BLOCK, COLS), i16), vmem((5, 3, 8, 128), f32),
            vmem((5, BLOCK, COLS), i16), vmem((5, 8, 128), f32),
            vmem((4, BLOCK, COLS), i16), vmem((4, 8, 128), f32),
            vmem((BLOCK, COLS), f32), vmem((4, BLOCK, 256), f32),
            dma((3,)), dma((3,)), dma((5, 2)), dma((5, 2)),
            dma((5, 2, 2)), dma((5, 3, 2)), dma((5, 2)), dma((4, 2)), dma((4,)), dma((4,)),
        ],
        compiler_params=pltpu.CompilerParams(
            collective_id=0, has_side_effects=True, vmem_limit_bytes=56 * 2**20
        ),
        cost_estimate=pl.CostEstimate(
            flops=2 * 2 * 5 * ROWS * COLS * DEPTH, bytes_accessed=2 * ROWS * DEPTH * 2, transcendentals=0
        ),
    )(fields, weights)


def per_device(
    velocity, elevation, panel_area, normal, block_map, waterline, heading, section, heading_table
):
    own_rows = velocity.shape[0]
    panels = velocity.shape[3]
    norm_scale = 1.0 / math.sqrt(panels * lax.axis_size("panel"))
    fields = jnp.concatenate([velocity, elevation[:, None]], axis=1).reshape(own_rows, -1)
    weights = panel_weights(panel_area, normal, block_map, waterline, section, norm_scale)
    weights = jnp.broadcast_to(weights[:, None, :], (4, 2, panels)).reshape(1, -1)
    out_rows = heading.shape[0] // lax.axis_size("panel")
    summed = reduced_product(fields, weights).reshape(out_rows, 2, own_rows)
    kinds = jnp.arange(heading_table.shape[0], dtype=jnp.int32)
    head_rows = lax.dynamic_slice_in_dim(heading, lax.axis_index("panel") * out_rows, out_rows, 0)
    head_cols = lax.dynamic_slice_in_dim(heading, lax.axis_index("tile") * own_rows, own_rows, 0)
    onehot_rows = (head_rows[:, None] == kinds[None, :]).astype(jnp.float32)
    onehot_cols = (kinds[:, None] == head_cols[None, :]).astype(jnp.float32)
    factor = jnp.dot(
        jnp.dot(onehot_rows, heading_table, precision=lax.Precision.HIGHEST),
        onehot_cols,
        precision=lax.Precision.HIGHEST,
    )
    return summed * factor[:, None, :]


def solution(mesh):
    placed = (
        P("tile", None, None, "panel"),
        P("tile", None, "panel"),
        P("panel"),
        P("panel"),
        P("panel"),
        P("panel"),
        P(),
        P(),
        P(),
    )
    return jax.shard_map(
        per_device, mesh=mesh, in_specs=placed, out_specs=P("panel", None, "tile"), check_vma=False
    )
```

```python
import functools
import math

import jax
import jax.numpy as jnp
from jax import lax
from jax.experimental import pallas as pl
from jax.experimental.pallas import tpu as pltpu
from jax.sharding import PartitionSpec as P

MESH = pl.DeviceIdType.MESH
ROWS = 512
DEPTH = 1024
COLS = 1024
HALF = 512
BLOCK = 128
LEVELS = 32000.0


def across_lanes(row, width):
    return jnp.concatenate([row] * (width // 128), axis=1)


def quantize(value):
    tiles = value.reshape(BLOCK // 8, 8, HALF)
    top = jnp.max(jnp.abs(tiles), axis=0)
    peak = top[:, :128]
    for k in range(1, HALF // 128):
        peak = jnp.maximum(peak, top[:, k * 128 : (k + 1) * 128])
    peak = jnp.maximum(peak, 1e-30)
    scaled = jnp.round(tiles * across_lanes(LEVELS / peak, HALF)[None]).astype(jnp.int32)
    return scaled.reshape(BLOCK, HALF).astype(jnp.int16), peak * (1.0 / LEVELS)


def dequantize(coded, scale):
    width = coded.shape[1]
    tiles = coded.astype(jnp.int32).astype(jnp.float32).reshape(BLOCK // 8, 8, width)
    return (tiles * across_lanes(scale, width)[None]).reshape(BLOCK, width)


def kernel(
    norm_scale,
    velocity_ref, elevation_ref, area_ref, normal_ref, map_ref, line_ref, heading_ref, section_ref, table_ref,
    out_ref,
    held, relay, across, own_hi, own_lo, across_hi, across_lo, part, core_in,
    y_out, y_out_scale, y_in, y_in_scale, z_out, z_out_scale, z_in, z_in_scale,
    total, m_out, m_out_scale, m_in, m_in_scale, factor,
    g_send, g_recv, c_send, c_recv, y_send, y_recv, z_send, z_recv, m_send, m_recv,
):
    panel, tile = lax.axis_index("panel"), lax.axis_index("tile")
    zh, y, c = panel // 8, (panel // 2) % 4, panel % 2
    a, x = tile // 4, tile % 4

    def at(zh_, y_, c_, a_, x_):
        return (zh_ * 8 + y_ * 2 + c_, a_ * 4 + x_)

    def copy(src, dst, send, recv, device):
        return pltpu.make_async_remote_copy(
            src_ref=src, dst_ref=dst, send_sem=send, recv_sem=recv, device_id=device, device_id_type=MESH
        )

    shifts = (0, 1, 2, 0, 1, 2)
    crossed = (False, False, False, True, True, True)
    shared = (False, False, True, True, False, True)

    def quadrant(p, half):
        return (half + (a if crossed[p] else x // 2)) % 2

    row_tile = panel // 4
    row_a, row_x = row_tile // 4, row_tile % 4
    shift = (row_x - x + 4) % 4
    same = row_a == a
    other = jnp.logical_not(same)
    owner = [jnp.logical_and(other if crossed[p] else same, shift == shifts[p]) for p in range(6)]
    kept = (y + jnp.where(same, x // 2, row_a)) % 2
    owns_all = jnp.logical_or(owner[0], jnp.logical_or(owner[1], owner[4]))
    owns_half = jnp.logical_or(owner[2], jnp.logical_or(owner[3], owner[5]))
    off_diagonal = row_tile != tile

    core_mate = at(zh, y, 1 - c, a, x)
    z_mate = at(zh, y, c, 1 - a, x)
    ahead, behind = at(zh, y, c, a, (x + 1) % 4), at(zh, y, c, a, (x + 3) % 4)
    y_mates = [at(zh, (y + k) % 4, c, a, x) for k in (1, 2, 3)]
    zh_mates = [at((zh + k) % 4, y, c, a, x) for k in (1, 2, 3)]
    far_mates = [at((zh + k) % 4, y, c, 1 - a, x) for k in (1, 2, 3)]
    mirrors = [(tile * 4 + q, row_tile) for q in range(4)]

    barrier = pltpu.get_barrier_semaphore()
    always = [core_mate, z_mate, ahead, behind] + y_mates + zh_mates + far_mates
    for mate in always:
        pl.semaphore_signal(barrier, inc=1, device_id=mate, device_id_type=MESH)

    @pl.when(off_diagonal)
    def _():
        for mate in mirrors:
            pl.semaphore_signal(barrier, inc=1, device_id=mate, device_id_type=MESH)

    held[0, :, :768] = velocity_ref[...]
    held[0, :, 768:] = elevation_ref[...]

    @pl.when(off_diagonal)
    def _():
        pl.semaphore_wait(barrier, len(always) + len(mirrors))

    @pl.when(jnp.logical_not(off_diagonal))
    def _():
        pl.semaphore_wait(barrier, len(always))

    low, high = pl.ds(0, 256), pl.ds(256, 256)
    first, second, short = pl.ds(352, 160), pl.ds(192, 160), pl.ds(0, 192)

    def gather(k, src, dst, device):
        return copy(src, dst, g_send.at[k], g_recv.at[k], device)

    next_low = gather(0, held.at[0, low], held.at[1, low], behind)
    next_high = gather(1, held.at[0, high], held.at[1, high], behind)
    across_low = gather(2, held.at[0, low], across.at[low], z_mate)
    across_high = gather(3, held.at[0, high], across.at[high], z_mate)
    relay_first = gather(4, held.at[0, first], relay.at[pl.ds(160, 160)], ahead)
    relay_second = gather(5, held.at[0, second], relay.at[pl.ds(0, 160)], ahead)
    pass_first = gather(6, relay.at[pl.ds(160, 160)], held.at[2, first], ahead)
    pass_second = gather(7, relay.at[pl.ds(0, 160)], held.at[2, second], ahead)
    pass_short = gather(8, held.at[1, short], held.at[2, short], behind)
    for each in (next_low, across_low, relay_first, next_high, across_high, relay_second):
        each.start()

    gain = jnp.zeros((1, BLOCK), jnp.float32)
    for k in range(section_ref.shape[0]):
        gain = gain + jnp.where(map_ref[...] == k, section_ref[k], 0.0)
    mode_value = normal_ref[...] * gain * norm_scale
    pressure = -0.5 * area_ref[...] * mode_value
    water_line = 0.5 * line_ref[...].astype(jnp.float32) * mode_value

    def right_side(src, hi, lo, blocks):
        for q in blocks:
            rows = pl.ds(q * BLOCK, BLOCK)
            direct = pl.ds(q * 2 * BLOCK, BLOCK)
            rotated = pl.ds(q * 2 * BLOCK + BLOCK, BLOCK)
            for k in range(DEPTH // 128):
                lanes = pl.ds(k * 128, 128)
                turned = pl.ds((k ^ 1) * 128, 128)
                value = src[rows, lanes].astype(jnp.float32) * (pressure if k < 6 else water_line)
                upper = value.astype(jnp.bfloat16)
                lower = (value - upper.astype(jnp.float32)).astype(jnp.bfloat16)
                hi[direct, lanes] = upper
                lo[direct, lanes] = lower
                hi[rotated, turned] = upper if k % 2 == 0 else -upper
                lo[rotated, turned] = lower if k % 2 == 0 else -lower

    def core_copy(p, half, side):
        rows = pl.ds(pl.multiple_of((1 - c) * BLOCK + half * 2 * BLOCK, BLOCK), BLOCK)
        return copy(
            part.at[p, side, rows], core_in.at[p, half], c_send.at[p, half], c_recv.at[p, half], core_mate
        ) if shared[p] else copy(
            part.at[p, side, rows], core_in.at[p + 6 * side, half],
            c_send.at[p + 6 * side, half], c_recv.at[p + 6 * side, half], core_mate,
        )

    def product(p, half, side):
        left = held.at[shifts[p]]
        hi, lo = (across_hi, across_lo) if crossed[p] else (own_hi, own_lo)
        rows = pl.ds(pl.multiple_of(half * 256, 256), 256)
        columns = pl.ds(pl.multiple_of(side * HALF, HALF), HALF)
        value = lax.dot_general(
            left[rows, :], hi[columns, :], (((1,), (1,)), ((), ())), preferred_element_type=jnp.float32
        )
        value += lax.dot_general(
            left[rows, :], lo[columns, :], (((1,), (1,)), ((), ())), preferred_element_type=jnp.float32
        )
        part[p, side, rows, :] = value
        core_copy(p, half, side).start()

    def mine(half):
        return pl.ds(pl.multiple_of(c * BLOCK + half * 2 * BLOCK, BLOCK), BLOCK)

    def y_half(p):
        return (x + shifts[p]) % 2

    def slot_of(p, side):
        return p if shared[p] else p + 6 * side

    def y_copies(p, half, side):
        target = y_half(p) * 2 + half
        source = (y - target + 4) % 4 - 1
        device = at(zh, target, c, a, x)
        k = slot_of(p, side)
        return [
            copy(y_out.at[k, half], y_in.at[k, source], y_send.at[k, half, 0], y_recv.at[k, source, 0], device),
            copy(
                y_out_scale.at[k, half], y_in_scale.at[k, source],
                y_send.at[k, half, 1], y_recv.at[k, source, 1], device,
            ),
        ]

    def start_y(p, half, side):
        core_copy(p, half, side).wait_recv()
        k = slot_of(p, side)
        value = part[p, side, mine(half), :] + core_in[k, half]
        local = y_half(p) * 2 + half == y

        @pl.when(local)
        def _():
            part[p, side, mine(half), :] = value

        @pl.when(jnp.logical_not(local))
        def _():
            y_out[k, half], y_out_scale[k, half] = quantize(value)
            for each in y_copies(p, half, side):
                each.start()

    def z_target(p):
        return a * 2 + ((x + shifts[p]) % 4) // 2

    def z_copies(p, side):
        device = at(z_target(p), y, c, 1 - a if crossed[p] else a, x)
        k = slot_of(p, side)
        return [
            copy(z_out.at[k], z_in.at[side, zh], z_send.at[k, 0], z_recv.at[side, zh, 0], device),
            copy(z_out_scale.at[k], z_in_scale.at[side, zh], z_send.at[k, 1], z_recv.at[side, zh, 1], device),
        ]

    def sides(p):
        return [quadrant(p, y % 2)] if shared[p] else [0, 1]

    def start_z(p):
        @pl.when(y_half(p) == y // 2)
        def _():
            for side in sides(p):
                k = slot_of(p, side)
                value = part[p, side, mine(y % 2), :]
                for source in range(3):
                    for n, (src, dst) in enumerate(
                        ((y_out.at[k, 0], y_in.at[k, source]), (y_out_scale.at[k, 0], y_in_scale.at[k, source]))
                    ):
                        copy(src, dst, y_send.at[k, 0, n], y_recv.at[k, source, n], y_mates[0]).wait_recv()
                    value += dequantize(y_in[k, source], y_in_scale[k, source])

                def send(value=value, side=side, k=k):
                    z_out[k], z_out_scale[k] = quantize(value)
                    for each in z_copies(p, side):
                        each.start()

                if crossed[p]:
                    send()
                else:
                    local = z_target(p) == zh

                    @pl.when(local)
                    def _(value=value, side=side):
                        total[side] = value

                    @pl.when(jnp.logical_not(local))
                    def _(send=send):
                        send()

    def mirror_copies(side):
        slot = panel % 4
        out = []
        for k in range(2):
            device = (tile * 4 + side * 2 + k, row_tile)
            columns = pl.ds(k * 256, 256)
            out.append(
                copy(m_out.at[side, :, columns], m_in.at[slot], m_send.at[side, k, 0], m_recv.at[slot, 0], device)
            )
            out.append(
                copy(m_out_scale.at[side], m_in_scale.at[slot], m_send.at[side, k, 1], m_recv.at[slot, 1], device)
            )
        return out

    def finish(p):
        @pl.when(owner[p])
        def _():
            for side in [kept] if shared[p] else [0, 1]:
                value = None if crossed[p] else total[side]
                for source in range(4) if crossed[p] else [(zh + k) % 4 for k in (1, 2, 3)]:
                    for n, (src, dst) in enumerate(
                        ((z_out.at[0], z_in.at[side, source]), (z_out_scale.at[0], z_in_scale.at[side, source]))
                    ):
                        copy(src, dst, z_send.at[0, n], z_recv.at[side, source, n], zh_mates[0]).wait_recv()
                    term = dequantize(z_in[side, source], z_in_scale[side, source])
                    value = term if value is None else value + term
                total[side] = value
                if p > 0:
                    m_out[side], m_out_scale[side] = quantize(value)
                    for each in mirror_copies(side):
                        each.start()

    right_side(held.at[0], own_hi, own_lo, range(4))
    for half in range(2):
        for side in range(2):
            product(0, half, side)
            if half:
                start_y(0, 0, side)

    kinds = lax.broadcasted_iota(jnp.int32, (8, BLOCK), 0)
    pick_rows = (kinds == heading_ref[pl.ds(panel, 1), :]).astype(jnp.float32)
    for k in range(4):
        pick_columns = (kinds == heading_ref[pl.ds(tile * 4 + k, 1), :]).astype(jnp.float32)
        by_row = jnp.dot(
            table_ref[...], pick_columns, precision=lax.Precision.HIGHEST, preferred_element_type=jnp.float32
        )
        factor[:, k * BLOCK : (k + 1) * BLOCK] = lax.dot_general(
            pick_rows, by_row, (((0,), (0,)), ((), ())),
            precision=lax.Precision.HIGHEST, preferred_element_type=jnp.float32,
        )

    start_y(0, 1, 0)
    start_y(0, 1, 1)
    relay_first.wait_recv()
    pass_first.start()
    next_low.wait_recv()
    product(1, 0, 0)
    product(1, 0, 1)
    across_low.wait_recv()
    right_side(across, across_hi, across_lo, (0, 1))
    start_y(1, 0, 0)
    product(3, a, 0)
    product(4, 0, 0)
    start_y(1, 0, 1)
    start_y(3, a, 0)
    start_y(4, 0, 0)
    relay_second.wait_recv()
    pass_second.start()
    start_z(0)
    next_high.wait_recv()
    pass_short.start()
    product(1, 1, 0)
    product(1, 1, 1)
    product(4, 1, 0)
    start_y(1, 1, 0)
    start_y(1, 1, 1)
    across_high.wait_recv()
    right_side(across, across_hi, across_lo, (2, 3))
    start_y(4, 1, 0)
    product(4, 0, 1)
    product(4, 1, 1)
    product(3, 1 - a, 1)
    start_y(4, 0, 1)
    start_y(4, 1, 1)
    start_y(3, 1 - a, 1)
    pass_first.wait_recv()
    pass_second.wait_recv()
    product(2, 1, quadrant(2, 1))
    product(5, 1, quadrant(5, 1))
    start_y(2, 1, quadrant(2, 1))
    start_y(5, 1, quadrant(5, 1))
    pass_short.wait_recv()
    product(2, 0, quadrant(2, 0))
    product(5, 0, quadrant(5, 0))
    start_y(2, 0, quadrant(2, 0))
    start_y(5, 0, quadrant(5, 0))
    for p in (3, 1, 4, 2, 5):
        start_z(p)
    for p in range(6):
        finish(p)

    def put(side, k, real, imaginary):
        columns = slice(side * 256 + k * 128, side * 256 + (k + 1) * 128)
        out_ref[:, columns] = real * factor[:, columns]
        out_ref[:, 512 + columns.start : 512 + columns.stop] = imaginary * factor[:, columns]

    for side in range(2):
        direct = jnp.logical_or(owns_all, jnp.logical_and(owns_half, kept == side))

        @pl.when(direct)
        def _(side=side):
            for k in range(2):
                put(side, k, total[side, :, k * 256 : k * 256 + 128], total[side, :, k * 256 + 128 : k * 256 + 256])

    for side in range(2):
        direct = jnp.logical_or(owns_all, jnp.logical_and(owns_half, kept == side))

        @pl.when(jnp.logical_not(direct))
        def _(side=side):
            for k in range(2):
                slot = side * 2 + k
                copy(
                    m_out.at[0, :, pl.ds(0, 256)], m_in.at[slot], m_send.at[0, 0, 0], m_recv.at[slot, 0], mirrors[slot]
                ).wait_recv()
                copy(
                    m_out_scale.at[0], m_in_scale.at[slot], m_send.at[0, 0, 1], m_recv.at[slot, 1], mirrors[slot]
                ).wait_recv()
                value = dequantize(m_in[slot], m_in_scale[slot])
                put(side, k, value[:, :128].T, -value[:, 128:].T)

    for each in (
        next_low, next_high, across_low, across_high, relay_first, relay_second, pass_first, pass_second, pass_short
    ):
        each.wait_send()
    for p in range(6):
        for half in range(2):
            for side in [quadrant(p, half)] if shared[p] else [0, 1]:
                core_copy(p, half, side).wait_send()

                @pl.when(y_half(p) * 2 + half != y)
                def _(p=p, half=half, side=side):
                    for each in y_copies(p, half, side):
                        each.wait_send()

        sends = y_half(p) == y // 2
        if not crossed[p]:
            sends = jnp.logical_and(sends, z_target(p) != zh)

        @pl.when(sends)
        def _(p=p):
            for side in sides(p):
                for each in z_copies(p, side):
                    each.wait_send()

        if p > 0:
            @pl.when(owner[p])
            def _(p=p):
                for side in [kept] if shared[p] else [0, 1]:
                    for each in mirror_copies(side):
                        each.wait_send()


def reduced_product(norm_scale, *operands):
    vmem, f32, bf16, i16 = pltpu.VMEM, jnp.float32, jnp.bfloat16, jnp.int16
    dma = pltpu.SemaphoreType.DMA
    whole = pl.BlockSpec(memory_space=vmem)
    return pl.pallas_call(
        functools.partial(kernel, norm_scale),
        out_shape=jax.ShapeDtypeStruct((BLOCK, COLS), f32),
        in_specs=[whole] * 7 + [pl.BlockSpec(memory_space=pltpu.SMEM), whole],
        out_specs=whole,
        scratch_shapes=[
            vmem((3, ROWS, DEPTH), bf16), vmem((320, DEPTH), bf16), vmem((ROWS, DEPTH), bf16),
            vmem((COLS, DEPTH), bf16), vmem((COLS, DEPTH), bf16),
            vmem((COLS, DEPTH), bf16), vmem((COLS, DEPTH), bf16),
            vmem((6, 2, ROWS, HALF), f32), vmem((12, 2, BLOCK, HALF), f32),
            vmem((12, 2, BLOCK, HALF), i16), vmem((12, 2, 8, 128), f32),
            vmem((12, 3, BLOCK, HALF), i16), vmem((12, 3, 8, 128), f32),
            vmem((12, BLOCK, HALF), i16), vmem((12, 8, 128), f32),
            vmem((2, 4, BLOCK, HALF), i16), vmem((2, 4, 8, 128), f32),
            vmem((2, BLOCK, HALF), f32),
            vmem((2, BLOCK, HALF), i16), vmem((2, 8, 128), f32),
            vmem((4, BLOCK, 256), i16), vmem((4, 8, 128), f32), vmem((BLOCK, ROWS), f32),
            dma((9,)), dma((9,)), dma((12, 2)), dma((12, 2)),
            dma((12, 2, 2)), dma((12, 3, 2)), dma((12, 2)), dma((2, 4, 2)), dma((2, 2, 2)), dma((4, 2)),
        ],
        compiler_params=pltpu.CompilerParams(
            collective_id=0, has_side_effects=True, vmem_limit_bytes=56 * 2**20
        ),
        cost_estimate=pl.CostEstimate(
            flops=2 * 2 * 5 * ROWS * COLS * DEPTH, bytes_accessed=2 * ROWS * DEPTH * 2, transcendentals=0
        ),
    )(*operands)


def per_device(
    velocity, elevation, panel_area, normal, block_map, waterline, heading, section, heading_table
):
    rows, panels = velocity.shape[0], velocity.shape[3]
    norm_scale = 1.0 / math.sqrt(panels * lax.axis_size("panel"))
    summed = reduced_product(
        norm_scale,
        velocity.reshape(rows, -1), elevation.reshape(rows, -1),
        panel_area[None], normal[None], block_map[None], waterline[None],
        heading.reshape(-1, panels), section, heading_table,
    )
    return summed.reshape(-1, 2, rows)


def solution(mesh):
    placed = (
        P("tile", None, None, "panel"),
        P("tile", None, "panel"),
        P("panel"),
        P("panel"),
        P("panel"),
        P("panel"),
        P(),
        P(),
        P(),
    )
    return jax.shard_map(
        per_device, mesh=mesh, in_specs=placed, out_specs=P("panel", None, "tile"), check_vma=False
    )
```

```python
import functools
import math

import jax
import jax.numpy as jnp
from jax import lax
from jax.experimental import pallas as pl
from jax.experimental.pallas import tpu as pltpu
from jax.sharding import PartitionSpec as P

MESH = pl.DeviceIdType.MESH
ROWS = 512
DEPTH = 1024
COLS = 1024
HALF = 512
BLOCK = 128
LEVELS = 32000.0


def across_lanes(row, width):
    return jnp.concatenate([row] * (width // 128), axis=1)


def encode(ref, value):
    width = value.shape[1]
    tiles = value.reshape(BLOCK // 8, 8, width)
    top = jnp.max(jnp.abs(tiles), axis=0)
    peak = top[:, :128]
    for k in range(1, width // 128):
        peak = jnp.maximum(peak, top[:, k * 128 : (k + 1) * 128])
    exponent = jnp.ceil(jnp.log2(jnp.maximum(peak, 1e-30) * (1.0 / LEVELS)))
    scaled = jnp.round(tiles * across_lanes(jnp.exp2(-exponent), width)[None]).astype(jnp.int32)
    coded = scaled.reshape(BLOCK, width).astype(jnp.int16)
    for k in range(width // 128):
        ref[pl.ds(k * BLOCK, BLOCK), :] = coded[:, k * 128 : (k + 1) * 128]
    whole = exponent.astype(jnp.int32)
    ref[pl.ds(width, 16), :] = jnp.concatenate([whole, whole], axis=0).astype(jnp.int16)


def decode(ref, width=HALF):
    exponent = ref[pl.ds(width, 16), :].astype(jnp.int32).astype(jnp.float32)[:8]
    step = jnp.exp2(exponent)[None]
    pieces = []
    for k in range(width // 128):
        piece = ref[pl.ds(k * BLOCK, BLOCK), :].astype(jnp.int32).astype(jnp.float32)
        pieces.append((piece.reshape(BLOCK // 8, 8, 128) * step).reshape(BLOCK, 128))
    return jnp.concatenate(pieces, axis=1)


def kernel(
    norm_scale,
    velocity_ref, elevation_ref, area_ref, normal_ref, map_ref, line_ref, heading_ref, section_ref, table_ref,
    out_ref,
    wide, held, relay, across, own_hi, own_lo, across_hi, across_lo, part, core_in,
    y_out, y_in, z_out, z_in, total, m_out, m_in, factor,
    g_send, g_recv, c_send, c_recv, y_send, y_recv, z_send, z_recv, m_send, m_recv,
):
    panel, tile = lax.axis_index("panel"), lax.axis_index("tile")
    zh, y, c = panel // 8, (panel // 2) % 4, panel % 2
    a, x = tile // 4, tile % 4

    def at(zh_, y_, c_, a_, x_):
        return (zh_ * 8 + y_ * 2 + c_, a_ * 4 + x_)

    def copy(src, dst, send, recv, device):
        return pltpu.make_async_remote_copy(
            src_ref=src, dst_ref=dst, send_sem=send, recv_sem=recv, device_id=device, device_id_type=MESH
        )

    shifts = (0, 1, 2, 0, 1, 2)
    crossed = (False, False, False, True, True, True)
    shared = (False, False, True, True, False, True)

    def quadrant(p, half):
        return (half + (a if crossed[p] else x // 2)) % 2

    row_tile = panel // 4
    row_a, row_x = row_tile // 4, row_tile % 4
    shift = (row_x - x + 4) % 4
    same = row_a == a
    other = jnp.logical_not(same)
    owner = [jnp.logical_and(other if crossed[p] else same, shift == shifts[p]) for p in range(6)]
    kept = (y + jnp.where(same, x // 2, row_a)) % 2
    owns_all = jnp.logical_or(owner[0], jnp.logical_or(owner[1], owner[4]))
    owns_half = jnp.logical_or(owner[2], jnp.logical_or(owner[3], owner[5]))
    off_diagonal = row_tile != tile

    core_mate = at(zh, y, 1 - c, a, x)
    z_mate = at(zh, y, c, 1 - a, x)
    ahead, behind = at(zh, y, c, a, (x + 1) % 4), at(zh, y, c, a, (x + 3) % 4)
    y_mates = [at(zh, (y + k) % 4, c, a, x) for k in (1, 2, 3)]
    zh_mates = [at((zh + k) % 4, y, c, a, x) for k in (1, 2, 3)]
    far_mates = [at((zh + k) % 4, y, c, 1 - a, x) for k in (1, 2, 3)]
    mirrors = [(tile * 4 + q, row_tile) for q in range(4)]

    barrier = pltpu.get_barrier_semaphore()
    always = [core_mate, z_mate, ahead, behind] + y_mates + zh_mates + far_mates
    for mate in always:
        pl.semaphore_signal(barrier, inc=1, device_id=mate, device_id_type=MESH)

    @pl.when(off_diagonal)
    def _():
        for mate in mirrors:
            pl.semaphore_signal(barrier, inc=1, device_id=mate, device_id_type=MESH)

    for part_rows in range(0, ROWS, 256):
        wide[pl.ds(part_rows * 6, 1536)] = velocity_ref[pl.ds(part_rows * 6, 1536)].astype(jnp.float32)
        wide[pl.ds(ROWS * 6 + part_rows * 2, 512)] = elevation_ref[pl.ds(part_rows * 2, 512)].astype(jnp.float32)
        for k in range(8):
            if k < 6:
                rows = pl.ds(part_rows * 6 + k, 256, stride=6)
            else:
                rows = pl.ds(ROWS * 6 + part_rows * 2 + k - 6, 256, stride=2)
            held[0, pl.ds(part_rows, 256), k * 128 : (k + 1) * 128] = wide[rows, :].astype(jnp.bfloat16)

    @pl.when(off_diagonal)
    def _():
        pl.semaphore_wait(barrier, len(always) + len(mirrors))

    @pl.when(jnp.logical_not(off_diagonal))
    def _():
        pl.semaphore_wait(barrier, len(always))

    low, high = pl.ds(0, 256), pl.ds(256, 256)
    first, second, short = pl.ds(352, 160), pl.ds(192, 160), pl.ds(0, 192)

    def gather(k, src, dst, device):
        return copy(src, dst, g_send.at[k], g_recv.at[k], device)

    nexts = [
        gather(9 + q, held.at[0, pl.ds(q * BLOCK, BLOCK)], held.at[1, pl.ds(q * BLOCK, BLOCK)], behind)
        for q in range(4)
    ]
    across_low = gather(2, held.at[0, low], across.at[low], z_mate)
    across_high = gather(3, held.at[0, high], across.at[high], z_mate)
    relay_first = gather(4, held.at[0, first], relay.at[pl.ds(160, 160)], ahead)
    relay_second = gather(5, held.at[0, second], relay.at[pl.ds(0, 160)], ahead)
    pass_first = gather(6, relay.at[pl.ds(160, 160)], held.at[2, first], ahead)
    pass_second = gather(7, relay.at[pl.ds(0, 160)], held.at[2, second], ahead)
    pass_short = gather(8, held.at[1, short], held.at[2, short], behind)
    for each in (
        nexts[0], across_low, relay_first, nexts[3], nexts[1], across_high, relay_second, nexts[2]
    ):
        each.start()

    gain = jnp.zeros((1, BLOCK), jnp.float32)
    for k in range(section_ref.shape[0]):
        gain = gain + jnp.where(map_ref[...] == k, section_ref[k], 0.0)
    mode_value = normal_ref[...] * gain * norm_scale
    pressure = -0.5 * area_ref[...] * mode_value
    water_line = 0.5 * line_ref[...].astype(jnp.float32) * mode_value

    def right_side(src, hi, lo, blocks):
        for q in blocks:
            rows = pl.ds(q * BLOCK, BLOCK)
            direct = pl.ds(q * 2 * BLOCK, BLOCK)
            rotated = pl.ds(q * 2 * BLOCK + BLOCK, BLOCK)
            for k in range(DEPTH // 128):
                lanes = pl.ds(k * 128, 128)
                turned = pl.ds((k ^ 1) * 128, 128)
                value = src[rows, lanes].astype(jnp.float32) * (pressure if k < 6 else water_line)
                upper = value.astype(jnp.bfloat16)
                lower = (value - upper.astype(jnp.float32)).astype(jnp.bfloat16)
                hi[direct, lanes] = upper
                lo[direct, lanes] = lower
                hi[rotated, turned] = upper if k % 2 == 0 else -upper
                lo[rotated, turned] = lower if k % 2 == 0 else -lower

    def core_copy(p, half, side):
        rows = pl.ds(pl.multiple_of((1 - c) * BLOCK + half * 2 * BLOCK, BLOCK), BLOCK)
        return copy(
            part.at[p, side, rows], core_in.at[p, half], c_send.at[p, half], c_recv.at[p, half], core_mate
        ) if shared[p] else copy(
            part.at[p, side, rows], core_in.at[p + 6 * side, half],
            c_send.at[p + 6 * side, half], c_recv.at[p + 6 * side, half], core_mate,
        )

    def multiply(p, rows, side):
        left = held.at[shifts[p]]
        hi, lo = (across_hi, across_lo) if crossed[p] else (own_hi, own_lo)
        columns = pl.ds(pl.multiple_of(side * HALF, HALF), HALF)
        value = lax.dot_general(
            left[rows, :], hi[columns, :], (((1,), (1,)), ((), ())), preferred_element_type=jnp.float32
        )
        value += lax.dot_general(
            left[rows, :], lo[columns, :], (((1,), (1,)), ((), ())), preferred_element_type=jnp.float32
        )
        part[p, side, rows, :] = value

    def product(p, half, side):
        multiply(p, pl.ds(pl.multiple_of(half * 256, 256), 256), side)
        core_copy(p, half, side).start()

    def product_of(p, q, side):
        multiply(p, pl.ds(q * BLOCK, BLOCK), side)

        @pl.when(c != q % 2)
        def _():
            core_copy(p, q // 2, side).start()

    def mine(half):
        return pl.ds(pl.multiple_of(c * BLOCK + half * 2 * BLOCK, BLOCK), BLOCK)

    def y_half(p):
        return (x + shifts[p]) % 2

    def slot_of(p, side):
        return p if shared[p] else p + 6 * side

    def y_copies(p, half, side):
        target = y_half(p) * 2 + half
        source = (y - target + 4) % 4 - 1
        device = at(zh, target, c, a, x)
        k = slot_of(p, side)
        return copy(y_out.at[k, half], y_in.at[k, source], y_send.at[k, half], y_recv.at[k, source], device)

    def start_y(p, half, side):
        core_copy(p, half, side).wait_recv()
        k = slot_of(p, side)
        value = part[p, side, mine(half), :] + core_in[k, half]
        local = y_half(p) * 2 + half == y

        @pl.when(local)
        def _():
            part[p, side, mine(half), :] = value

        @pl.when(jnp.logical_not(local))
        def _():
            encode(y_out.at[k, half], value)
            y_copies(p, half, side).start()

    def start_y_of(p, q, side):
        @pl.when(c == q % 2)
        def _():
            start_y(p, q // 2, side)

    def z_target(p):
        return a * 2 + ((x + shifts[p]) % 4) // 2

    def z_copies(p, side):
        device = at(z_target(p), y, c, 1 - a if crossed[p] else a, x)
        k = slot_of(p, side)
        return copy(z_out.at[k], z_in.at[side, zh], z_send.at[k], z_recv.at[side, zh], device)

    def sides(p):
        return [quadrant(p, y % 2)] if shared[p] else [0, 1]

    def start_z(p, when=None):
        mine_now = y_half(p) == y // 2
        if when is not None:
            mine_now = jnp.logical_and(mine_now, when)

        @pl.when(mine_now)
        def _():
            for side in sides(p):
                k = slot_of(p, side)
                value = part[p, side, mine(y % 2), :]
                for source in range(3):
                    copy(
                        y_out.at[k, 0], y_in.at[k, source], y_send.at[k, 0], y_recv.at[k, source], y_mates[0]
                    ).wait_recv()
                    value += decode(y_in.at[k, source])

                def send(value=value, side=side, k=k):
                    encode(z_out.at[k], value)
                    z_copies(p, side).start()

                if crossed[p]:
                    send()
                else:
                    local = z_target(p) == zh

                    @pl.when(local)
                    def _(value=value, side=side):
                        total[side] = value

                    @pl.when(jnp.logical_not(local))
                    def _(send=send):
                        send()

    def mirror_copies(side):
        slot = panel % 4
        return [
            copy(
                m_out.at[side, k], m_in.at[slot], m_send.at[side, k], m_recv.at[slot],
                (tile * 4 + side * 2 + k, row_tile),
            )
            for k in range(2)
        ]

    def finish(p):
        @pl.when(owner[p])
        def _():
            for side in [kept] if shared[p] else [0, 1]:
                value = None if crossed[p] else total[side]
                for source in range(4) if crossed[p] else [(zh + k) % 4 for k in (1, 2, 3)]:
                    copy(
                        z_out.at[0], z_in.at[side, source], z_send.at[0], z_recv.at[side, source], zh_mates[0]
                    ).wait_recv()
                    term = decode(z_in.at[side, source])
                    value = term if value is None else value + term
                total[side] = value
                if p > 0:
                    for k, each in enumerate(mirror_copies(side)):
                        encode(m_out.at[side, k], value[:, k * 256 : (k + 1) * 256])
                        each.start()

    def wait_gathers_and_core():
        for each in (
            *nexts, across_low, across_high, relay_first, relay_second, pass_first, pass_second, pass_short
        ):
            each.wait_send()
        for p in range(6):
            for half in range(2):
                for side in [quadrant(p, half)] if shared[p] else [0, 1]:
                    core_copy(p, half, side).wait_send()

    def wait_y(pairs):
        for p in pairs:
            for half in range(2):
                for side in [quadrant(p, half)] if shared[p] else [0, 1]:
                    @pl.when(y_half(p) * 2 + half != y)
                    def _(p=p, half=half, side=side):
                        y_copies(p, half, side).wait_send()

    right_side(held.at[0], own_hi, own_lo, range(4))
    for half in range(2):
        for side in range(2):
            product(0, half, side)
    start_y(0, 0, 0)
    start_y(0, 0, 1)
    kinds = lax.broadcasted_iota(jnp.int32, (8, BLOCK), 0)
    pick_rows = (kinds == heading_ref[pl.ds(panel, 1), :]).astype(jnp.float32)
    for k in range(4):
        pick_columns = (kinds == heading_ref[pl.ds(tile * 4 + k, 1), :]).astype(jnp.float32)
        by_row = jnp.dot(
            table_ref[...], pick_columns, precision=lax.Precision.HIGHEST, preferred_element_type=jnp.float32
        )
        factor[:, k * BLOCK : (k + 1) * BLOCK] = lax.dot_general(
            pick_rows, by_row, (((0,), (0,)), ((), ())),
            precision=lax.Precision.HIGHEST, preferred_element_type=jnp.float32,
        )
    start_y(0, 1, 0)
    start_y(0, 1, 1)
    nexts[0].wait_recv()
    product_of(1, 0, 0)
    product_of(1, 0, 1)
    relay_first.wait_recv()
    pass_first.start()
    start_y_of(1, 0, 0)
    start_y_of(1, 0, 1)
    nexts[3].wait_recv()
    product_of(1, 3, 0)
    product_of(1, 3, 1)
    across_low.wait_recv()
    right_side(across, across_hi, across_lo, (0, 1))
    start_y_of(1, 3, 0)
    start_y_of(1, 3, 1)
    product_of(4, 0, 0)
    product_of(4, 3, 0)
    product(3, a, 0)
    start_y_of(4, 0, 0)
    start_y_of(4, 3, 0)
    relay_second.wait_recv()
    pass_second.start()
    start_y(3, a, 0)
    nexts[1].wait_recv()
    pass_short.start()
    product_of(1, 1, 0)
    product_of(1, 1, 1)
    product_of(4, 1, 0)
    start_z(0)
    start_y_of(1, 1, 0)
    start_y_of(1, 1, 1)
    start_y_of(4, 1, 0)
    start_z(1, y % 2 == c)
    nexts[2].wait_recv()
    product_of(1, 2, 0)
    product_of(1, 2, 1)
    product_of(4, 2, 0)
    across_high.wait_recv()
    right_side(across, across_hi, across_lo, (2, 3))
    start_y_of(1, 2, 0)
    start_y_of(1, 2, 1)
    product(4, 0, 1)
    start_y_of(4, 2, 0)
    product(4, 1, 1)
    product(3, 1 - a, 1)
    start_y(4, 0, 1)
    start_y(4, 1, 1)
    pass_first.wait_recv()
    pass_second.wait_recv()
    product(2, 1, quadrant(2, 1))
    start_y(3, 1 - a, 1)
    product(5, 1, quadrant(5, 1))
    pass_short.wait_recv()
    product(2, 0, quadrant(2, 0))
    start_y(2, 1, quadrant(2, 1))
    product(5, 0, quadrant(5, 0))
    start_y(5, 1, quadrant(5, 1))
    start_y(2, 0, quadrant(2, 0))
    start_y(5, 0, quadrant(5, 0))
    start_z(3, y % 2 == a)
    start_z(1, y % 2 != c)
    start_z(3, y % 2 != a)
    start_z(4)
    wait_gathers_and_core()
    finish(1)
    finish(4)
    start_z(2)
    start_z(5)
    wait_y(range(6))
    for p in (3, 2, 5, 0):
        finish(p)

    def put(side, k, real, imaginary):
        q = side * 2 + k
        scale = factor[:, q * 128 : (q + 1) * 128]
        out_ref[pl.ds(q * 2, BLOCK, stride=8), :] = real * scale
        out_ref[pl.ds(q * 2 + 1, BLOCK, stride=8), :] = imaginary * scale

    for side in range(2):
        direct = jnp.logical_or(owns_all, jnp.logical_and(owns_half, kept == side))

        @pl.when(direct)
        def _(side=side):
            for k in range(2):
                put(side, k, total[side, :, k * 256 : k * 256 + 128], total[side, :, k * 256 + 128 : k * 256 + 256])

    for side in range(2):
        direct = jnp.logical_or(owns_all, jnp.logical_and(owns_half, kept == side))

        @pl.when(jnp.logical_not(direct))
        def _(side=side):
            for k in range(2):
                slot = side * 2 + k
                copy(m_out.at[0, 0], m_in.at[slot], m_send.at[0, 0], m_recv.at[slot], mirrors[slot]).wait_recv()
                value = decode(m_in.at[slot], 256)
                put(side, k, value[:, :128].T, -value[:, 128:].T)

    for p in range(6):
        sends = y_half(p) == y // 2
        if not crossed[p]:
            sends = jnp.logical_and(sends, z_target(p) != zh)

        @pl.when(sends)
        def _(p=p):
            for side in sides(p):
                z_copies(p, side).wait_send()

        if p > 0:
            @pl.when(owner[p])
            def _(p=p):
                for side in [kept] if shared[p] else [0, 1]:
                    for each in mirror_copies(side):
                        each.wait_send()


def reduced_product(norm_scale, *operands):
    vmem, f32, bf16, i16 = pltpu.VMEM, jnp.float32, jnp.bfloat16, jnp.int16
    dma = pltpu.SemaphoreType.DMA
    whole = pl.BlockSpec(memory_space=vmem)
    return pl.pallas_call(
        functools.partial(kernel, norm_scale),
        out_shape=jax.ShapeDtypeStruct((BLOCK * COLS // 128, 128), f32),
        in_specs=[whole] * 7 + [pl.BlockSpec(memory_space=pltpu.SMEM), whole],
        out_specs=whole,
        scratch_shapes=[
            vmem((8 * ROWS, 128), f32), vmem((3, ROWS, DEPTH), bf16), vmem((320, DEPTH), bf16), vmem((ROWS, DEPTH), bf16),
            vmem((COLS, DEPTH), bf16), vmem((COLS, DEPTH), bf16),
            vmem((COLS, DEPTH), bf16), vmem((COLS, DEPTH), bf16),
            vmem((6, 2, ROWS, HALF), f32), vmem((12, 2, BLOCK, HALF), f32),
            vmem((12, 2, HALF + 16, 128), i16), vmem((12, 3, HALF + 16, 128), i16),
            vmem((12, HALF + 16, 128), i16), vmem((2, 4, HALF + 16, 128), i16),
            vmem((2, BLOCK, HALF), f32),
            vmem((2, 2, 272, 128), i16), vmem((4, 272, 128), i16), vmem((BLOCK, ROWS), f32),
            dma((13,)), dma((13,)), dma((12, 2)), dma((12, 2)),
            dma((12, 2)), dma((12, 3)), dma((12,)), dma((2, 4)), dma((2, 2)), dma((4,)),
        ],
        compiler_params=pltpu.CompilerParams(
            collective_id=0, has_side_effects=True, vmem_limit_bytes=56 * 2**20
        ),
        cost_estimate=pl.CostEstimate(
            flops=2 * 2 * 5 * ROWS * COLS * DEPTH, bytes_accessed=2 * ROWS * DEPTH * 2, transcendentals=0
        ),
    )(*operands)


def per_device(
    velocity, elevation, panel_area, normal, block_map, waterline, heading, section, heading_table
):
    rows, panels = velocity.shape[0], velocity.shape[3]
    norm_scale = 1.0 / math.sqrt(panels * lax.axis_size("panel"))
    summed = reduced_product(
        norm_scale,
        velocity.reshape(-1, panels), elevation.reshape(-1, panels),
        panel_area[None], normal[None], block_map[None], waterline[None],
        heading.reshape(-1, panels), section, heading_table,
    )
    return summed.reshape(-1, rows // 128, 2, 128).transpose(0, 2, 1, 3).reshape(-1, 2, rows)


def solution(mesh):
    placed = (
        P("tile", None, None, "panel"),
        P("tile", None, "panel"),
        P("panel"),
        P("panel"),
        P("panel"),
        P("panel"),
        P(),
        P(),
        P(),
    )
    return jax.shard_map(
        per_device, mesh=mesh, in_specs=placed, out_specs=P("panel", None, "tile"), check_vma=False
    )
```

```python
import functools
import math

import jax
import jax.numpy as jnp
from jax import lax
from jax.experimental import pallas as pl
from jax.experimental.pallas import tpu as pltpu
from jax.sharding import PartitionSpec as P

MESH = pl.DeviceIdType.MESH
ROWS = 512
DEPTH = 1024
COLS = 1024
HALF = 512
BLOCK = 128
LEVELS = 32000.0


def across_lanes(row, width):
    return jnp.concatenate([row] * (width // 128), axis=1)


def encode(ref, value):
    width = value.shape[1]
    tiles = value.reshape(BLOCK // 8, 8, width)
    top = jnp.max(jnp.abs(tiles), axis=0)
    peak = top[:, :128]
    for k in range(1, width // 128):
        peak = jnp.maximum(peak, top[:, k * 128 : (k + 1) * 128])
    exponent = jnp.ceil(jnp.log2(jnp.maximum(peak, 1e-30) * (1.0 / LEVELS)))
    scaled = jnp.round(tiles * across_lanes(jnp.exp2(-exponent), width)[None]).astype(jnp.int32)
    coded = scaled.reshape(BLOCK, width).astype(jnp.int16)
    for k in range(width // 128):
        ref[pl.ds(k * BLOCK, BLOCK), :] = coded[:, k * 128 : (k + 1) * 128]
    whole = exponent.astype(jnp.int32)
    ref[pl.ds(width, 16), :] = jnp.concatenate([whole, whole], axis=0).astype(jnp.int16)


def decode(ref, width=HALF):
    exponent = ref[pl.ds(width, 16), :].astype(jnp.int32).astype(jnp.float32)[:8]
    step = jnp.exp2(exponent)[None]
    pieces = []
    for k in range(width // 128):
        piece = ref[pl.ds(k * BLOCK, BLOCK), :].astype(jnp.int32).astype(jnp.float32)
        pieces.append((piece.reshape(BLOCK // 8, 8, 128) * step).reshape(BLOCK, 128))
    return jnp.concatenate(pieces, axis=1)


def kernel(
    norm_scale,
    velocity_ref, elevation_ref, area_ref, normal_ref, map_ref, line_ref, heading_ref, section_ref, table_ref,
    out_ref,
    wide, held, relay, across, own_hi, own_lo, across_hi, across_lo, part, core_in,
    y_out, y_in, z_out, z_in, total, m_out, m_in, factor,
    g_send, g_recv, c_send, c_recv, y_send, y_recv, z_send, z_recv, m_send, m_recv,
):
    panel, tile = lax.axis_index("panel"), lax.axis_index("tile")
    zh, y, c = panel // 8, (panel // 2) % 4, panel % 2
    a, x = tile // 4, tile % 4

    def at(zh_, y_, c_, a_, x_):
        return (zh_ * 8 + y_ * 2 + c_, a_ * 4 + x_)

    def copy(src, dst, send, recv, device):
        return pltpu.make_async_remote_copy(
            src_ref=src, dst_ref=dst, send_sem=send, recv_sem=recv, device_id=device, device_id_type=MESH
        )

    shifts = (0, 1, 2, 0, 1, 2)
    crossed = (False, False, False, True, True, True)
    shared = (False, False, True, True, False, True)

    def quadrant(p, half):
        return (half + (a if crossed[p] else x // 2)) % 2

    row_tile = panel // 4
    row_a, row_x = row_tile // 4, row_tile % 4
    shift = (row_x - x + 4) % 4
    same = row_a == a
    other = jnp.logical_not(same)
    owner = [jnp.logical_and(other if crossed[p] else same, shift == shifts[p]) for p in range(6)]
    kept = (y + jnp.where(same, x // 2, row_a)) % 2
    owns_all = jnp.logical_or(owner[0], jnp.logical_or(owner[1], owner[4]))
    owns_half = jnp.logical_or(owner[2], jnp.logical_or(owner[3], owner[5]))
    off_diagonal = row_tile != tile

    core_mate = at(zh, y, 1 - c, a, x)
    z_mate = at(zh, y, c, 1 - a, x)
    ahead, behind = at(zh, y, c, a, (x + 1) % 4), at(zh, y, c, a, (x + 3) % 4)
    y_mates = [at(zh, (y + k) % 4, c, a, x) for k in (1, 2, 3)]
    zh_mates = [at((zh + k) % 4, y, c, a, x) for k in (1, 2, 3)]
    far_mates = [at((zh + k) % 4, y, c, 1 - a, x) for k in (1, 2, 3)]
    mirrors = [(tile * 4 + q, row_tile) for q in range(4)]

    barrier = pltpu.get_barrier_semaphore()
    always = [core_mate, z_mate, ahead, behind] + y_mates + zh_mates + far_mates
    for mate in always:
        pl.semaphore_signal(barrier, inc=1, device_id=mate, device_id_type=MESH)

    @pl.when(off_diagonal)
    def _():
        for mate in mirrors:
            pl.semaphore_signal(barrier, inc=1, device_id=mate, device_id_type=MESH)

    for part_rows in range(0, ROWS, 256):
        wide[pl.ds(part_rows * 6, 1536)] = velocity_ref[pl.ds(part_rows * 6, 1536)].astype(jnp.float32)
        wide[pl.ds(ROWS * 6 + part_rows * 2, 512)] = elevation_ref[pl.ds(part_rows * 2, 512)].astype(jnp.float32)
        for k in range(8):
            if k < 6:
                rows = pl.ds(part_rows * 6 + k, 256, stride=6)
            else:
                rows = pl.ds(ROWS * 6 + part_rows * 2 + k - 6, 256, stride=2)
            held[0, pl.ds(part_rows, 256), k * 128 : (k + 1) * 128] = wide[rows, :].astype(jnp.bfloat16)

    @pl.when(off_diagonal)
    def _():
        pl.semaphore_wait(barrier, len(always) + len(mirrors))

    @pl.when(jnp.logical_not(off_diagonal))
    def _():
        pl.semaphore_wait(barrier, len(always))

    low, high = pl.ds(0, 256), pl.ds(256, 256)
    first, second, short = pl.ds(352, 160), pl.ds(192, 160), pl.ds(0, 192)

    def gather(k, src, dst, device):
        return copy(src, dst, g_send.at[k], g_recv.at[k], device)

    nexts = [
        gather(9 + q, held.at[0, pl.ds(q * BLOCK, BLOCK)], held.at[1, pl.ds(q * BLOCK, BLOCK)], behind)
        for q in range(4)
    ]
    across_low = gather(2, held.at[0, low], across.at[low], z_mate)
    across_high = gather(3, held.at[0, high], across.at[high], z_mate)
    relay_first = gather(4, held.at[0, first], relay.at[pl.ds(160, 160)], ahead)
    relay_second = gather(5, held.at[0, second], relay.at[pl.ds(0, 160)], ahead)
    pass_first = gather(6, relay.at[pl.ds(160, 160)], held.at[2, first], ahead)
    pass_second = gather(7, relay.at[pl.ds(0, 160)], held.at[2, second], ahead)
    pass_short = gather(8, held.at[1, short], held.at[2, short], behind)
    for each in (
        nexts[0], across_low, relay_first, nexts[3], nexts[1], across_high, relay_second, nexts[2]
    ):
        each.start()

    gain = jnp.zeros((1, BLOCK), jnp.float32)
    for k in range(section_ref.shape[0]):
        gain = gain + jnp.where(map_ref[...] == k, section_ref[k], 0.0)
    mode_value = normal_ref[...] * gain * norm_scale
    pressure = -0.5 * area_ref[...] * mode_value
    water_line = 0.5 * line_ref[...].astype(jnp.float32) * mode_value

    def right_side(src, hi, lo, blocks):
        for q in blocks:
            rows = pl.ds(q * BLOCK, BLOCK)
            direct = pl.ds(q * 2 * BLOCK, BLOCK)
            rotated = pl.ds(q * 2 * BLOCK + BLOCK, BLOCK)
            for k in range(DEPTH // 128):
                lanes = pl.ds(k * 128, 128)
                turned = pl.ds((k ^ 1) * 128, 128)
                value = src[rows, lanes].astype(jnp.float32) * (pressure if k < 6 else water_line)
                upper = value.astype(jnp.bfloat16)
                lower = (value - upper.astype(jnp.float32)).astype(jnp.bfloat16)
                hi[direct, lanes] = upper
                lo[direct, lanes] = lower
                hi[rotated, turned] = upper if k % 2 == 0 else -upper
                lo[rotated, turned] = lower if k % 2 == 0 else -lower

    def core_copy(p, half, side):
        rows = pl.ds(pl.multiple_of((1 - c) * BLOCK + half * 2 * BLOCK, BLOCK), BLOCK)
        return copy(
            part.at[p, side, rows], core_in.at[p, half], c_send.at[p, half], c_recv.at[p, half], core_mate
        ) if shared[p] else copy(
            part.at[p, side, rows], core_in.at[p + 6 * side, half],
            c_send.at[p + 6 * side, half], c_recv.at[p + 6 * side, half], core_mate,
        )

    def multiply(p, rows, side):
        left = held.at[shifts[p]]
        hi, lo = (across_hi, across_lo) if crossed[p] else (own_hi, own_lo)
        columns = pl.ds(pl.multiple_of(side * HALF, HALF), HALF)
        value = lax.dot_general(
            left[rows, :], hi[columns, :], (((1,), (1,)), ((), ())), preferred_element_type=jnp.float32
        )
        value += lax.dot_general(
            left[rows, :], lo[columns, :], (((1,), (1,)), ((), ())), preferred_element_type=jnp.float32
        )
        part[p, side, rows, :] = value

    def product(p, half, side):
        multiply(p, pl.ds(pl.multiple_of(half * 256, 256), 256), side)
        core_copy(p, half, side).start()

    def product_of(p, q, side):
        multiply(p, pl.ds(q * BLOCK, BLOCK), side)

        @pl.when(c != q % 2)
        def _():
            core_copy(p, q // 2, side).start()

    def mine(half):
        return pl.ds(pl.multiple_of(c * BLOCK + half * 2 * BLOCK, BLOCK), BLOCK)

    def y_half(p):
        return (x + shifts[p]) % 2

    def slot_of(p, side):
        return p if shared[p] else p + 6 * side

    def y_copies(p, half, side):
        target = y_half(p) * 2 + half
        source = (y - target + 4) % 4 - 1
        device = at(zh, target, c, a, x)
        k = slot_of(p, side)
        return copy(y_out.at[k, half], y_in.at[k, source], y_send.at[k, half], y_recv.at[k, source], device)

    def start_y(p, half, side):
        core_copy(p, half, side).wait_recv()
        k = slot_of(p, side)
        value = part[p, side, mine(half), :] + core_in[k, half]
        local = y_half(p) * 2 + half == y

        @pl.when(local)
        def _():
            part[p, side, mine(half), :] = value

        @pl.when(jnp.logical_not(local))
        def _():
            encode(y_out.at[k, half], value)
            y_copies(p, half, side).start()

    def start_y_of(p, q, side):
        @pl.when(c == q % 2)
        def _():
            start_y(p, q // 2, side)

    def z_target(p):
        return a * 2 + ((x + shifts[p]) % 4) // 2

    def z_copies(p, side):
        device = at(z_target(p), y, c, 1 - a if crossed[p] else a, x)
        k = slot_of(p, side)
        return copy(z_out.at[k], z_in.at[side, zh], z_send.at[k], z_recv.at[side, zh], device)

    def sides(p):
        return [quadrant(p, y % 2)] if shared[p] else [0, 1]

    def start_z(p, when=None, only=None):
        mine_now = y_half(p) == y // 2
        if when is not None:
            mine_now = jnp.logical_and(mine_now, when)

        @pl.when(mine_now)
        def _():
            for side in sides(p) if only is None else [only]:
                k = slot_of(p, side)
                value = part[p, side, mine(y % 2), :]
                for source in range(3):
                    copy(
                        y_out.at[k, 0], y_in.at[k, source], y_send.at[k, 0], y_recv.at[k, source], y_mates[0]
                    ).wait_recv()
                    value += decode(y_in.at[k, source])

                def send(value=value, side=side, k=k):
                    encode(z_out.at[k], value)
                    z_copies(p, side).start()

                if crossed[p]:
                    send()
                else:
                    local = z_target(p) == zh

                    @pl.when(local)
                    def _(value=value, side=side):
                        total[side] = value

                    @pl.when(jnp.logical_not(local))
                    def _(send=send):
                        send()

    def mirror_copies(side):
        slot = panel % 4
        return [
            copy(
                m_out.at[side, k], m_in.at[slot], m_send.at[side, k], m_recv.at[slot],
                (tile * 4 + side * 2 + k, row_tile),
            )
            for k in range(2)
        ]

    def finish(p, when=None):
        @pl.when(owner[p] if when is None else jnp.logical_and(owner[p], when))
        def _():
            for side in [kept] if shared[p] else [0, 1]:
                value = None if crossed[p] else total[side]
                for source in range(4) if crossed[p] else [(zh + k) % 4 for k in (1, 2, 3)]:
                    copy(
                        z_out.at[0], z_in.at[side, source], z_send.at[0], z_recv.at[side, source], zh_mates[0]
                    ).wait_recv()
                    term = decode(z_in.at[side, source])
                    value = term if value is None else value + term
                total[side] = value
                if p > 0:
                    for k, each in enumerate(mirror_copies(side)):
                        encode(m_out.at[side, k], value[:, k * 256 : (k + 1) * 256])
                        each.start()

    def wait_gathers_and_core():
        for each in (
            *nexts, across_low, across_high, relay_first, relay_second, pass_first, pass_second, pass_short
        ):
            each.wait_send()
        for p in range(6):
            for half in range(2):
                for side in [quadrant(p, half)] if shared[p] else [0, 1]:
                    core_copy(p, half, side).wait_send()

    def wait_y(pairs):
        for p in pairs:
            for half in range(2):
                for side in [quadrant(p, half)] if shared[p] else [0, 1]:
                    @pl.when(y_half(p) * 2 + half != y)
                    def _(p=p, half=half, side=side):
                        y_copies(p, half, side).wait_send()

    right_side(held.at[0], own_hi, own_lo, range(4))
    for half in range(2):
        for side in range(2):
            product(0, half, side)
    start_y(0, 0, 0)
    start_y(0, 0, 1)
    kinds = lax.broadcasted_iota(jnp.int32, (8, BLOCK), 0)
    pick_rows = (kinds == heading_ref[pl.ds(panel, 1), :]).astype(jnp.float32)
    for k in range(4):
        pick_columns = (kinds == heading_ref[pl.ds(tile * 4 + k, 1), :]).astype(jnp.float32)
        by_row = jnp.dot(
            table_ref[...], pick_columns, precision=lax.Precision.HIGHEST, preferred_element_type=jnp.float32
        )
        factor[:, k * BLOCK : (k + 1) * BLOCK] = lax.dot_general(
            pick_rows, by_row, (((0,), (0,)), ((), ())),
            precision=lax.Precision.HIGHEST, preferred_element_type=jnp.float32,
        )
    start_y(0, 1, 0)
    start_y(0, 1, 1)
    nexts[0].wait_recv()
    product_of(1, 0, 0)
    product_of(1, 0, 1)
    relay_first.wait_recv()
    pass_first.start()
    start_y_of(1, 0, 0)
    start_y_of(1, 0, 1)
    nexts[3].wait_recv()
    product_of(1, 3, 0)
    product_of(1, 3, 1)
    across_low.wait_recv()
    right_side(across, across_hi, across_lo, (0, 1))
    start_y_of(1, 3, 0)
    start_y_of(1, 3, 1)
    product_of(4, 0, 0)
    product_of(4, 3, 0)
    product(3, a, 0)
    start_y_of(4, 0, 0)
    start_y_of(4, 3, 0)
    relay_second.wait_recv()
    pass_second.start()
    start_y(3, a, 0)
    nexts[1].wait_recv()
    pass_short.start()
    product_of(1, 1, 0)
    product_of(1, 1, 1)
    product_of(4, 1, 0)
    start_z(0)
    start_y_of(1, 1, 0)
    start_y_of(1, 1, 1)
    start_y_of(4, 1, 0)
    early = y % 2 == c
    late = jnp.logical_not(early)
    start_z(1, early)
    start_z(4, early, 0)
    nexts[2].wait_recv()
    product_of(1, 2, 0)
    product_of(1, 2, 1)
    across_high.wait_recv()
    right_side(across, across_hi, across_lo, (2, 3))
    product(3, 1 - a, 1)
    start_y_of(1, 2, 0)
    start_y_of(1, 2, 1)
    product_of(4, 2, 0)
    product(4, 0, 1)
    start_y(3, 1 - a, 1)
    product(4, 1, 1)
    start_y_of(4, 2, 0)
    start_y(4, 0, 1)
    start_y(4, 1, 1)
    pass_first.wait_recv()
    pass_second.wait_recv()
    product(5, 1, quadrant(5, 1))
    product(2, 1, quadrant(2, 1))
    start_y(5, 1, quadrant(5, 1))
    pass_short.wait_recv()
    product(5, 0, quadrant(5, 0))
    start_y(2, 1, quadrant(2, 1))
    product(2, 0, quadrant(2, 0))
    start_y(5, 0, quadrant(5, 0))
    start_y(2, 0, quadrant(2, 0))
    start_z(3, y % 2 == a)
    start_z(1, jnp.logical_and(late, y % 2 == 0))
    start_z(4, jnp.logical_and(late, y % 2 == 0), 0)
    start_z(1, jnp.logical_and(late, y % 2 == 1))
    start_z(4, jnp.logical_and(late, y % 2 == 1), 0)
    start_z(3, y % 2 != a)
    start_z(4, None, 1)
    wait_gathers_and_core()
    finish(1)
    finish(4)
    start_z(5)
    start_z(2)
    wait_y(range(6))
    for p in (5, 2, 3, 0):
        finish(p)

    def put(side, k, real, imaginary):
        q = side * 2 + k
        scale = factor[:, q * 128 : (q + 1) * 128]
        out_ref[pl.ds(q * 2, BLOCK, stride=8), :] = real * scale
        out_ref[pl.ds(q * 2 + 1, BLOCK, stride=8), :] = imaginary * scale

    for side in range(2):
        direct = jnp.logical_or(owns_all, jnp.logical_and(owns_half, kept == side))

        @pl.when(direct)
        def _(side=side):
            for k in range(2):
                put(side, k, total[side, :, k * 256 : k * 256 + 128], total[side, :, k * 256 + 128 : k * 256 + 256])

    for side in range(2):
        direct = jnp.logical_or(owns_all, jnp.logical_and(owns_half, kept == side))

        @pl.when(jnp.logical_not(direct))
        def _(side=side):
            for k in range(2):
                slot = side * 2 + k
                copy(m_out.at[0, 0], m_in.at[slot], m_send.at[0, 0], m_recv.at[slot], mirrors[slot]).wait_recv()
                value = decode(m_in.at[slot], 256)
                put(side, k, value[:, :128].T, -value[:, 128:].T)

    for p in range(6):
        sends = y_half(p) == y // 2
        if not crossed[p]:
            sends = jnp.logical_and(sends, z_target(p) != zh)

        @pl.when(sends)
        def _(p=p):
            for side in sides(p):
                z_copies(p, side).wait_send()

        if p > 0:
            @pl.when(owner[p])
            def _(p=p):
                for side in [kept] if shared[p] else [0, 1]:
                    for each in mirror_copies(side):
                        each.wait_send()


def reduced_product(norm_scale, *operands):
    vmem, f32, bf16, i16 = pltpu.VMEM, jnp.float32, jnp.bfloat16, jnp.int16
    dma = pltpu.SemaphoreType.DMA
    whole = pl.BlockSpec(memory_space=vmem)
    return pl.pallas_call(
        functools.partial(kernel, norm_scale),
        out_shape=vmem((BLOCK * COLS // 128, 128), f32),
        in_specs=[whole] * 7 + [pl.BlockSpec(memory_space=pltpu.SMEM), whole],
        out_specs=whole,
        scratch_shapes=[
            vmem((8 * ROWS, 128), f32), vmem((3, ROWS, DEPTH), bf16), vmem((320, DEPTH), bf16), vmem((ROWS, DEPTH), bf16),
            vmem((COLS, DEPTH), bf16), vmem((COLS, DEPTH), bf16),
            vmem((COLS, DEPTH), bf16), vmem((COLS, DEPTH), bf16),
            vmem((6, 2, ROWS, HALF), f32), vmem((12, 2, BLOCK, HALF), f32),
            vmem((12, 2, HALF + 16, 128), i16), vmem((12, 3, HALF + 16, 128), i16),
            vmem((12, HALF + 16, 128), i16), vmem((2, 4, HALF + 16, 128), i16),
            vmem((2, BLOCK, HALF), f32),
            vmem((2, 2, 272, 128), i16), vmem((4, 272, 128), i16), vmem((BLOCK, ROWS), f32),
            dma((13,)), dma((13,)), dma((12, 2)), dma((12, 2)),
            dma((12, 2)), dma((12, 3)), dma((12,)), dma((2, 4)), dma((2, 2)), dma((4,)),
        ],
        compiler_params=pltpu.CompilerParams(
            collective_id=0, has_side_effects=True, vmem_limit_bytes=56 * 2**20
        ),
        cost_estimate=pl.CostEstimate(
            flops=2 * 2 * 5 * ROWS * COLS * DEPTH, bytes_accessed=2 * ROWS * DEPTH * 2, transcendentals=0
        ),
    )(*operands)


def per_device(
    velocity, elevation, panel_area, normal, block_map, waterline, heading, section, heading_table
):
    rows, panels = velocity.shape[0], velocity.shape[3]
    norm_scale = 1.0 / math.sqrt(panels * lax.axis_size("panel"))
    summed = reduced_product(
        norm_scale,
        velocity.reshape(-1, panels), elevation.reshape(-1, panels),
        panel_area[None], normal[None], block_map[None], waterline[None],
        heading.reshape(-1, panels), section, heading_table,
    )
    return summed.reshape(-1, rows // 128, 2, 128).transpose(0, 2, 1, 3).reshape(-1, 2, rows)


def solution(mesh):
    placed = (
        P("tile", None, None, "panel"),
        P("tile", None, "panel"),
        P("panel"),
        P("panel"),
        P("panel"),
        P("panel"),
        P(),
        P(),
        P(),
    )
    return jax.shard_map(
        per_device, mesh=mesh, in_specs=placed, out_specs=P("panel", None, "tile"), check_vma=False
    )
```

```python
import functools
import math

import jax
import jax.numpy as jnp
from jax import lax
from jax.experimental import pallas as pl
from jax.experimental.pallas import tpu as pltpu
from jax.sharding import PartitionSpec as P

MESH = pl.DeviceIdType.MESH
ROWS = 512
DEPTH = 1024
COLS = 1024
HALF = 512
BLOCK = 128
LEVELS = 32000.0


def across_lanes(row, width):
    return jnp.concatenate([row] * (width // 128), axis=1)


def encode(ref, value):
    width = value.shape[1]
    tiles = value.reshape(BLOCK // 8, 8, width)
    top = jnp.max(jnp.abs(tiles), axis=0)
    peak = top[:, :128]
    for k in range(1, width // 128):
        peak = jnp.maximum(peak, top[:, k * 128 : (k + 1) * 128])
    exponent = jnp.ceil(jnp.log2(jnp.maximum(peak, 1e-30) * (1.0 / LEVELS)))
    scaled = jnp.round(tiles * across_lanes(jnp.exp2(-exponent), width)[None]).astype(jnp.int32)
    coded = scaled.reshape(BLOCK, width).astype(jnp.int16)
    for k in range(width // 128):
        ref[pl.ds(k * BLOCK, BLOCK), :] = coded[:, k * 128 : (k + 1) * 128]
    whole = exponent.astype(jnp.int32)
    ref[pl.ds(width, 16), :] = jnp.concatenate([whole, whole], axis=0).astype(jnp.int16)


def decode(ref, width=HALF):
    exponent = ref[pl.ds(width, 16), :].astype(jnp.int32).astype(jnp.float32)[:8]
    step = jnp.exp2(exponent)[None]
    pieces = []
    for k in range(width // 128):
        piece = ref[pl.ds(k * BLOCK, BLOCK), :].astype(jnp.int32).astype(jnp.float32)
        pieces.append((piece.reshape(BLOCK // 8, 8, 128) * step).reshape(BLOCK, 128))
    return jnp.concatenate(pieces, axis=1)


def kernel(
    norm_scale,
    velocity_ref, elevation_ref, area_ref, normal_ref, map_ref, line_ref, heading_ref, section_ref, table_ref,
    out_ref,
    wide, held, relay, across, own_hi, own_lo, across_hi, across_lo, part, core_in,
    y_out, y_in, z_out, z_in, total, m_out, m_in, factor,
    g_send, g_recv, c_send, c_recv, y_send, y_recv, z_send, z_recv, m_send, m_recv,
):
    panel, tile = lax.axis_index("panel"), lax.axis_index("tile")
    zh, y, c = panel // 8, (panel // 2) % 4, panel % 2
    a, x = tile // 4, tile % 4

    def at(zh_, y_, c_, a_, x_):
        return (zh_ * 8 + y_ * 2 + c_, a_ * 4 + x_)

    def copy(src, dst, send, recv, device):
        return pltpu.make_async_remote_copy(
            src_ref=src, dst_ref=dst, send_sem=send, recv_sem=recv, device_id=device, device_id_type=MESH
        )

    shifts = (0, 1, 2, 0, 1, 2)
    crossed = (False, False, False, True, True, True)
    shared = (False, False, True, True, False, True)

    def quadrant(p, half):
        return (half + (a if crossed[p] else x // 2)) % 2

    row_tile = panel // 4
    row_a, row_x = row_tile // 4, row_tile % 4
    shift = (row_x - x + 4) % 4
    same = row_a == a
    other = jnp.logical_not(same)
    owner = [jnp.logical_and(other if crossed[p] else same, shift == shifts[p]) for p in range(6)]
    kept = (y + jnp.where(same, x // 2, row_a)) % 2
    owns_all = jnp.logical_or(owner[0], jnp.logical_or(owner[1], owner[4]))
    owns_half = jnp.logical_or(owner[2], jnp.logical_or(owner[3], owner[5]))
    off_diagonal = row_tile != tile

    core_mate = at(zh, y, 1 - c, a, x)
    z_mate = at(zh, y, c, 1 - a, x)
    ahead, behind = at(zh, y, c, a, (x + 1) % 4), at(zh, y, c, a, (x + 3) % 4)
    y_mates = [at(zh, (y + k) % 4, c, a, x) for k in (1, 2, 3)]
    zh_mates = [at((zh + k) % 4, y, c, a, x) for k in (1, 2, 3)]
    far_mates = [at((zh + k) % 4, y, c, 1 - a, x) for k in (1, 2, 3)]
    mirrors = [(tile * 4 + q, row_tile) for q in range(4)]

    barrier = pltpu.get_barrier_semaphore()
    always = [core_mate, z_mate, ahead, behind] + y_mates + zh_mates + far_mates
    for mate in always:
        pl.semaphore_signal(barrier, inc=1, device_id=mate, device_id_type=MESH)

    @pl.when(off_diagonal)
    def _():
        for mate in mirrors:
            pl.semaphore_signal(barrier, inc=1, device_id=mate, device_id_type=MESH)

    def lay_out(part_rows):
        wide[pl.ds(part_rows * 6, 1536)] = velocity_ref[pl.ds(part_rows * 6, 1536)].astype(jnp.float32)
        wide[pl.ds(ROWS * 6 + part_rows * 2, 512)] = elevation_ref[pl.ds(part_rows * 2, 512)].astype(jnp.float32)
        for k in range(8):
            if k < 6:
                rows = pl.ds(part_rows * 6 + k, 256, stride=6)
            else:
                rows = pl.ds(ROWS * 6 + part_rows * 2 + k - 6, 256, stride=2)
            held[0, pl.ds(part_rows, 256), k * 128 : (k + 1) * 128] = wide[rows, :].astype(jnp.bfloat16)

    lay_out(0)

    @pl.when(off_diagonal)
    def _():
        pl.semaphore_wait(barrier, len(always) + len(mirrors))

    @pl.when(jnp.logical_not(off_diagonal))
    def _():
        pl.semaphore_wait(barrier, len(always))

    low = pl.ds(0, 256)
    first, second, short = pl.ds(352, 160), pl.ds(192, 160), pl.ds(0, 192)

    def gather(k, src, dst, device):
        return copy(src, dst, g_send.at[k], g_recv.at[k], device)

    nexts = [
        gather(9 + q, held.at[0, pl.ds(q * BLOCK, BLOCK)], held.at[1, pl.ds(q * BLOCK, BLOCK)], behind)
        for q in range(4)
    ]
    across_low = gather(2, held.at[0, low], across.at[low], z_mate)
    third, fourth = pl.ds(256, 128), pl.ds(384, 128)
    across_third = gather(3, held.at[0, third], across.at[third], z_mate)
    across_fourth = gather(13, held.at[0, fourth], across.at[fourth], z_mate)
    relay_first = gather(4, held.at[0, first], relay.at[pl.ds(160, 160)], ahead)
    relay_second = gather(5, held.at[0, second], relay.at[pl.ds(0, 160)], ahead)
    pass_first = gather(6, relay.at[pl.ds(160, 160)], held.at[2, first], ahead)
    pass_second = gather(7, relay.at[pl.ds(0, 160)], held.at[2, second], ahead)
    pass_short = gather(8, held.at[1, short], held.at[2, short], behind)
    nexts[0].start()
    across_low.start()
    lay_out(256)
    for each in (relay_first, nexts[3], nexts[1], across_third, relay_second, nexts[2], across_fourth):
        each.start()

    gain = jnp.zeros((1, BLOCK), jnp.float32)
    for k in range(section_ref.shape[0]):
        gain = gain + jnp.where(map_ref[...] == k, section_ref[k], 0.0)
    mode_value = normal_ref[...] * gain * norm_scale
    pressure = -0.5 * area_ref[...] * mode_value
    water_line = 0.5 * line_ref[...].astype(jnp.float32) * mode_value

    def right_side(src, hi, lo, blocks):
        for q in blocks:
            rows = pl.ds(q * BLOCK, BLOCK)
            direct = pl.ds(q * 2 * BLOCK, BLOCK)
            rotated = pl.ds(q * 2 * BLOCK + BLOCK, BLOCK)
            for k in range(DEPTH // 128):
                lanes = pl.ds(k * 128, 128)
                turned = pl.ds((k ^ 1) * 128, 128)
                value = src[rows, lanes].astype(jnp.float32) * (pressure if k < 6 else water_line)
                upper = value.astype(jnp.bfloat16)
                lower = (value - upper.astype(jnp.float32)).astype(jnp.bfloat16)
                hi[direct, lanes] = upper
                lo[direct, lanes] = lower
                hi[rotated, turned] = upper if k % 2 == 0 else -upper
                lo[rotated, turned] = lower if k % 2 == 0 else -lower

    def core_copy(p, half, side):
        rows = pl.ds(pl.multiple_of((1 - c) * BLOCK + half * 2 * BLOCK, BLOCK), BLOCK)
        return copy(
            part.at[p, side, rows], core_in.at[p, half], c_send.at[p, half], c_recv.at[p, half], core_mate
        ) if shared[p] else copy(
            part.at[p, side, rows], core_in.at[p + 6 * side, half],
            c_send.at[p + 6 * side, half], c_recv.at[p + 6 * side, half], core_mate,
        )

    def multiply(p, rows, side):
        left = held.at[shifts[p]]
        hi, lo = (across_hi, across_lo) if crossed[p] else (own_hi, own_lo)
        columns = pl.ds(pl.multiple_of(side * HALF, HALF), HALF)
        value = lax.dot_general(
            left[rows, :], hi[columns, :], (((1,), (1,)), ((), ())), preferred_element_type=jnp.float32
        )
        value += lax.dot_general(
            left[rows, :], lo[columns, :], (((1,), (1,)), ((), ())), preferred_element_type=jnp.float32
        )
        part[p, side, rows, :] = value

    def product(p, half, side):
        multiply(p, pl.ds(pl.multiple_of(half * 256, 256), 256), side)
        core_copy(p, half, side).start()

    def product_of(p, q, side):
        multiply(p, pl.ds(q * BLOCK, BLOCK), side)

        @pl.when(c != q % 2)
        def _():
            core_copy(p, q // 2, side).start()

    def mine(half):
        return pl.ds(pl.multiple_of(c * BLOCK + half * 2 * BLOCK, BLOCK), BLOCK)

    def y_half(p):
        return (x + shifts[p]) % 2

    def slot_of(p, side):
        return p if shared[p] else p + 6 * side

    def y_copies(p, half, side):
        target = y_half(p) * 2 + half
        source = (y - target + 4) % 4 - 1
        device = at(zh, target, c, a, x)
        k = slot_of(p, side)
        return copy(y_out.at[k, half], y_in.at[k, source], y_send.at[k, half], y_recv.at[k, source], device)

    def start_y(p, half, side):
        core_copy(p, half, side).wait_recv()
        k = slot_of(p, side)
        value = part[p, side, mine(half), :] + core_in[k, half]
        local = y_half(p) * 2 + half == y

        @pl.when(local)
        def _():
            part[p, side, mine(half), :] = value

        @pl.when(jnp.logical_not(local))
        def _():
            encode(y_out.at[k, half], value)
            y_copies(p, half, side).start()

    def start_y_of(p, q, side):
        @pl.when(c == q % 2)
        def _():
            start_y(p, q // 2, side)

    def z_target(p):
        return a * 2 + ((x + shifts[p]) % 4) // 2

    def z_copies(p, side):
        device = at(z_target(p), y, c, 1 - a if crossed[p] else a, x)
        k = slot_of(p, side)
        return copy(z_out.at[k], z_in.at[side, zh], z_send.at[k], z_recv.at[side, zh], device)

    def sides(p):
        return [quadrant(p, y % 2)] if shared[p] else [0, 1]

    def start_z(p, when=None, only=None):
        mine_now = y_half(p) == y // 2
        if when is not None:
            mine_now = jnp.logical_and(mine_now, when)

        @pl.when(mine_now)
        def _():
            for side in sides(p) if only is None else [only]:
                k = slot_of(p, side)
                value = part[p, side, mine(y % 2), :]
                for source in range(3):
                    copy(
                        y_out.at[k, 0], y_in.at[k, source], y_send.at[k, 0], y_recv.at[k, source], y_mates[0]
                    ).wait_recv()
                    value += decode(y_in.at[k, source])

                def send(value=value, side=side, k=k):
                    encode(z_out.at[k], value)
                    z_copies(p, side).start()

                if crossed[p]:
                    send()
                else:
                    local = z_target(p) == zh

                    @pl.when(local)
                    def _(value=value, side=side):
                        total[side] = value

                    @pl.when(jnp.logical_not(local))
                    def _(send=send):
                        send()

    def mirror_copies(side):
        slot = panel % 4
        return [
            copy(
                m_out.at[side, k], m_in.at[slot], m_send.at[side, k], m_recv.at[slot],
                (tile * 4 + side * 2 + k, row_tile),
            )
            for k in range(2)
        ]

    def finish(p, when=None):
        @pl.when(owner[p] if when is None else jnp.logical_and(owner[p], when))
        def _():
            for side in [kept] if shared[p] else [0, 1]:
                value = None if crossed[p] else total[side]
                for source in range(4) if crossed[p] else [(zh + k) % 4 for k in (1, 2, 3)]:
                    copy(
                        z_out.at[0], z_in.at[side, source], z_send.at[0], z_recv.at[side, source], zh_mates[0]
                    ).wait_recv()
                    term = decode(z_in.at[side, source])
                    value = term if value is None else value + term
                total[side] = value
                if p > 0:
                    for k, each in enumerate(mirror_copies(side)):
                        encode(m_out.at[side, k], value[:, k * 256 : (k + 1) * 256])
                        each.start()

    def wait_gathers_and_core():
        for each in (
            *nexts, across_low, across_third, across_fourth, relay_first, relay_second, pass_first, pass_second, pass_short
        ):
            each.wait_send()
        for p in range(6):
            for half in range(2):
                for side in [quadrant(p, half)] if shared[p] else [0, 1]:
                    core_copy(p, half, side).wait_send()

    def wait_y(pairs):
        for p in pairs:
            for half in range(2):
                for side in [quadrant(p, half)] if shared[p] else [0, 1]:
                    @pl.when(y_half(p) * 2 + half != y)
                    def _(p=p, half=half, side=side):
                        y_copies(p, half, side).wait_send()

    right_side(held.at[0], own_hi, own_lo, range(4))
    for half in range(2):
        for side in range(2):
            product(0, half, side)
    start_y(0, 0, 0)
    start_y(0, 0, 1)
    kinds = lax.broadcasted_iota(jnp.int32, (8, BLOCK), 0)
    pick_rows = (kinds == heading_ref[pl.ds(panel, 1), :]).astype(jnp.float32)
    for k in range(4):
        pick_columns = (kinds == heading_ref[pl.ds(tile * 4 + k, 1), :]).astype(jnp.float32)
        by_row = jnp.dot(
            table_ref[...], pick_columns, precision=lax.Precision.HIGHEST, preferred_element_type=jnp.float32
        )
        factor[:, k * BLOCK : (k + 1) * BLOCK] = lax.dot_general(
            pick_rows, by_row, (((0,), (0,)), ((), ())),
            precision=lax.Precision.HIGHEST, preferred_element_type=jnp.float32,
        )
    start_y(0, 1, 0)
    start_y(0, 1, 1)
    nexts[0].wait_recv()
    product_of(1, 0, 0)
    product_of(1, 0, 1)
    relay_first.wait_recv()
    pass_first.start()
    start_y_of(1, 0, 0)
    start_y_of(1, 0, 1)
    nexts[3].wait_recv()
    product_of(1, 3, 0)
    product_of(1, 3, 1)
    across_low.wait_recv()
    right_side(across, across_hi, across_lo, (0, 1))
    start_y_of(1, 3, 0)
    start_y_of(1, 3, 1)
    product_of(4, 0, 0)
    product_of(4, 3, 0)
    product(3, a, 0)
    start_y_of(4, 0, 0)
    start_y_of(4, 3, 0)
    relay_second.wait_recv()
    pass_second.start()
    start_y(3, a, 0)
    nexts[1].wait_recv()
    pass_short.start()
    product_of(1, 1, 0)
    product_of(1, 1, 1)
    product_of(4, 1, 0)
    start_z(0)
    start_y_of(1, 1, 0)
    start_y_of(1, 1, 1)
    start_y_of(4, 1, 0)
    early = y % 2 == c
    late = jnp.logical_not(early)
    start_z(1, early)
    start_z(4, early, 0)
    across_third.wait_recv()
    right_side(across, across_hi, across_lo, (2,))
    nexts[2].wait_recv()
    product_of(1, 2, 0)
    product_of(1, 2, 1)
    across_fourth.wait_recv()
    right_side(across, across_hi, across_lo, (3,))
    product(3, 1 - a, 1)
    start_y_of(1, 2, 0)
    start_y_of(1, 2, 1)
    product_of(4, 2, 0)
    product(4, 0, 1)
    start_y(3, 1 - a, 1)
    product(4, 1, 1)
    start_y_of(4, 2, 0)
    start_y(4, 0, 1)
    start_y(4, 1, 1)
    pass_first.wait_recv()
    pass_second.wait_recv()
    product(5, 1, quadrant(5, 1))
    product(2, 1, quadrant(2, 1))
    start_y(5, 1, quadrant(5, 1))
    pass_short.wait_recv()
    product(5, 0, quadrant(5, 0))
    start_y(2, 1, quadrant(2, 1))
    product(2, 0, quadrant(2, 0))
    start_y(5, 0, quadrant(5, 0))
    start_y(2, 0, quadrant(2, 0))
    start_z(3, y % 2 == a)
    start_z(1, jnp.logical_and(late, y % 2 == 0))
    start_z(4, jnp.logical_and(late, y % 2 == 0), 0)
    start_z(1, jnp.logical_and(late, y % 2 == 1))
    start_z(4, jnp.logical_and(late, y % 2 == 1), 0)
    start_z(3, y % 2 != a)
    start_z(4, None, 1)
    wait_gathers_and_core()
    finish(1)
    finish(4)
    start_z(5)
    start_z(2)
    wait_y(range(6))
    for p in (5, 2, 3, 0):
        finish(p)

    def put(side, k, real, imaginary):
        q = side * 2 + k
        scale = factor[:, q * 128 : (q + 1) * 128]
        out_ref[pl.ds(q * 2, BLOCK, stride=8), :] = real * scale
        out_ref[pl.ds(q * 2 + 1, BLOCK, stride=8), :] = imaginary * scale

    for side in range(2):
        direct = jnp.logical_or(owns_all, jnp.logical_and(owns_half, kept == side))

        @pl.when(direct)
        def _(side=side):
            for k in range(2):
                put(side, k, total[side, :, k * 256 : k * 256 + 128], total[side, :, k * 256 + 128 : k * 256 + 256])

    for side in range(2):
        direct = jnp.logical_or(owns_all, jnp.logical_and(owns_half, kept == side))

        @pl.when(jnp.logical_not(direct))
        def _(side=side):
            for k in range(2):
                slot = side * 2 + k
                copy(m_out.at[0, 0], m_in.at[slot], m_send.at[0, 0], m_recv.at[slot], mirrors[slot]).wait_recv()
                value = decode(m_in.at[slot], 256)
                put(side, k, value[:, :128].T, -value[:, 128:].T)

    for p in range(6):
        sends = y_half(p) == y // 2
        if not crossed[p]:
            sends = jnp.logical_and(sends, z_target(p) != zh)

        @pl.when(sends)
        def _(p=p):
            for side in sides(p):
                z_copies(p, side).wait_send()

        if p > 0:
            @pl.when(owner[p])
            def _(p=p):
                for side in [kept] if shared[p] else [0, 1]:
                    for each in mirror_copies(side):
                        each.wait_send()


def reduced_product(norm_scale, *operands):
    vmem, f32, bf16, i16 = pltpu.VMEM, jnp.float32, jnp.bfloat16, jnp.int16
    dma = pltpu.SemaphoreType.DMA
    whole = pl.BlockSpec(memory_space=vmem)
    return pl.pallas_call(
        functools.partial(kernel, norm_scale),
        out_shape=vmem((BLOCK * COLS // 128, 128), f32),
        in_specs=[whole] * 7 + [pl.BlockSpec(memory_space=pltpu.SMEM), whole],
        out_specs=whole,
        scratch_shapes=[
            vmem((8 * ROWS, 128), f32), vmem((3, ROWS, DEPTH), bf16), vmem((320, DEPTH), bf16), vmem((ROWS, DEPTH), bf16),
            vmem((COLS, DEPTH), bf16), vmem((COLS, DEPTH), bf16),
            vmem((COLS, DEPTH), bf16), vmem((COLS, DEPTH), bf16),
            vmem((6, 2, ROWS, HALF), f32), vmem((12, 2, BLOCK, HALF), f32),
            vmem((12, 2, HALF + 16, 128), i16), vmem((12, 3, HALF + 16, 128), i16),
            vmem((12, HALF + 16, 128), i16), vmem((2, 4, HALF + 16, 128), i16),
            vmem((2, BLOCK, HALF), f32),
            vmem((2, 2, 272, 128), i16), vmem((4, 272, 128), i16), vmem((BLOCK, ROWS), f32),
            dma((14,)), dma((14,)), dma((12, 2)), dma((12, 2)),
            dma((12, 2)), dma((12, 3)), dma((12,)), dma((2, 4)), dma((2, 2)), dma((4,)),
        ],
        compiler_params=pltpu.CompilerParams(
            collective_id=0, has_side_effects=True, vmem_limit_bytes=56 * 2**20
        ),
        cost_estimate=pl.CostEstimate(
            flops=2 * 2 * 5 * ROWS * COLS * DEPTH, bytes_accessed=2 * ROWS * DEPTH * 2, transcendentals=0
        ),
    )(*operands)


def per_device(
    velocity, elevation, panel_area, normal, block_map, waterline, heading, section, heading_table
):
    rows, panels = velocity.shape[0], velocity.shape[3]
    norm_scale = 1.0 / math.sqrt(panels * lax.axis_size("panel"))
    summed = reduced_product(
        norm_scale,
        velocity.reshape(-1, panels), elevation.reshape(-1, panels),
        panel_area[None], normal[None], block_map[None], waterline[None],
        heading.reshape(-1, panels), section, heading_table,
    )
    return summed.reshape(-1, rows // 128, 2, 128).transpose(0, 2, 1, 3).reshape(-1, 2, rows)


def solution(mesh):
    placed = (
        P("tile", None, None, "panel"),
        P("tile", None, "panel"),
        P("panel"),
        P("panel"),
        P("panel"),
        P("panel"),
        P(),
        P(),
        P(),
    )
    return jax.shard_map(
        per_device, mesh=mesh, in_specs=placed, out_specs=P("panel", None, "tile"), check_vma=False
    )
```
